256 devices in a mesh: row: 8 (over y, core), col: 32 (over z, x).
Axes of the slice: x: 4, y: 4, z: 8, core: 2. Of those that a mesh axis runs over, the one named last changes fastest.
Arguments:
- diag_inverse: float32 [2, 2048, 2048], P(None, 'row', 'col'), may hold values from -0.09375 to 0.09375
- panel_rhs: float32 [2, 2048, 128], P(None, 'col'), may hold values from -6 to 6
- factor_slab: bfloat16 [2, 131072, 2048], P(None, ('row', 'col')), may hold values from -0.09375 to 0.09375
- pending_rhs: float32 [2, 131072, 128], P(None, ('row', 'col')), may hold values from -6 to 6
- solved_prev: bfloat16 [2, 65536, 128], P(None, ('row', 'col')), may hold values from -6 to 6
- modes_prev: bfloat16 [65536, 128], P(('row', 'col')), may hold values from -0.0234375 to 0.0234375
- modes_panel: bfloat16 [2048, 128], P(('row', 'col')), may hold values from -0.0234375 to 0.0234375
Outputs:
- panel_solution: float32 [2, 2048, 128], P(None, ('row', 'col'))
- updated_rhs: float32 [2, 131072, 128], P(None, ('row', 'col'))
- modal_forces: float32 [2, 128, 128], replicated
The draws below stay inside these ranges and needn't reach their ends.
All inputs are finite; a program needn't handle non-finite values.
Results may differ from the reference program's by a relative error of at most 0.002.
Values may be sent and summed in bfloat16 or wider, within the bound.
No kernel may reach another device: no remote copies, remote signals or barrier semaphores. Data moves between devices by JAX's collectives and lax.ppermute only.
A program may use at most 64 MiB of HBM per device.

```python
import jax
import jax.numpy as jnp
from jax import lax

PANEL = 2048
MODES = 128
UP_ROWS = 131072
DONE_ROWS = 65536


def shard_levels(own_key, dims, shards, smallest, high):
    gain = 1.0
    for axis_at, shards_of in shards:
        draws = jax.random.uniform(jax.random.fold_in(jax.random.fold_in(own_key, 6), axis_at), (shards_of,), jnp.float32, smallest / len(shards), high / len(shards))
        gain = gain * jnp.repeat(jnp.exp(draws), dims[axis_at] // shards_of).reshape((-1,) + (1,) * (len(dims) - 1 - axis_at))
    return gain


def noise(own_key, shape, width, most, cuts=(), held_as=jnp.bfloat16):
    factor_of = shard_levels(own_key, shape, cuts, -0.22, 0.18) if cuts else 1.0
    result = jax.random.normal(own_key, shape, jnp.float32) * width * factor_of
    return jnp.minimum(jnp.maximum(result, -most), most).astype(held_as)


def setup_inputs(seed: int = 0) -> dict:
    key_of = jax.random.split(jax.random.key(seed), 8)
    return {
        "diag_inverse": noise(key_of[0], (2, PANEL, PANEL), (2 * PANEL) ** -0.5, 0.09375, ((1, 8), (2, 32)), jnp.float32),
        "panel_rhs": noise(key_of[1], (2, PANEL, MODES), 1.0, 6.0, ((1, 32),), jnp.float32),
        "factor_slab": noise(key_of[2], (2, UP_ROWS, PANEL), (2 * PANEL) ** -0.5, 0.09375, ((1, 256),)),
        "pending_rhs": noise(key_of[3], (2, UP_ROWS, MODES), 1.0, 6.0, ((1, 256),), jnp.float32),
        "solved_prev": noise(key_of[4], (2, DONE_ROWS, MODES), 1.0, 6.0, ((1, 256),)),
        "modes_prev": noise(key_of[5], (DONE_ROWS, MODES), (DONE_ROWS + PANEL) ** -0.5, 0.0234375, ((0, 256),)),
        "modes_panel": noise(key_of[6], (PANEL, MODES), (DONE_ROWS + PANEL) ** -0.5, 0.0234375, ((0, 256),)),
    }


def reference(diag_inverse, panel_rhs, factor_slab, pending_rhs, solved_prev, modes_prev, modes_panel):
    highest = lax.Precision.HIGHEST
    real_part = jnp.dot(diag_inverse[0], panel_rhs[0], precision=highest, preferred_element_type=jnp.float32) - jnp.dot(diag_inverse[1], panel_rhs[1], precision=highest, preferred_element_type=jnp.float32)
    imag_part = jnp.dot(diag_inverse[0], panel_rhs[1], precision=highest, preferred_element_type=jnp.float32) + jnp.dot(diag_inverse[1], panel_rhs[0], precision=highest, preferred_element_type=jnp.float32)
    panel_solution = jnp.stack([real_part, imag_part])
    rounded = panel_solution.astype(jnp.bfloat16)
    joined = jnp.concatenate([rounded[0], rounded[1]], axis=1)
    real_acc = jnp.dot(factor_slab[0], joined, preferred_element_type=jnp.float32)
    imag_acc = jnp.dot(factor_slab[1], joined, preferred_element_type=jnp.float32)
    update_real = real_acc[:, :MODES] - imag_acc[:, MODES:]
    update_imag = real_acc[:, MODES:] + imag_acc[:, :MODES]
    updated_rhs = jnp.stack([pending_rhs[0] - update_real, pending_rhs[1] - update_imag])
    earlier = jnp.einsum("sk,csm->ckm", modes_prev.astype(jnp.float32), solved_prev.astype(jnp.float32))
    latest = jnp.einsum("sk,csm->ckm", modes_panel.astype(jnp.float32), rounded.astype(jnp.float32))
    modal_forces = earlier + latest
    return panel_solution, updated_rhs, modal_forces
```

```python
import jax
import jax.numpy as jnp
from jax import lax
from jax.sharding import Mesh, PartitionSpec as P

F32 = jnp.float32
BF16 = jnp.bfloat16
COL = ("z", "x")
SWAP = [(0, 1), (1, 0)]


def flipped(value, bits):
    return lax.ppermute(value, "y", [(i, i ^ bits) for i in range(4)])


def on_device(
    diag_inverse, panel_rhs, factor_slab, pending_rhs, solved_prev, modes_prev, modes_panel
):
    width = panel_rhs.shape[2]
    own = modes_panel.shape[0]
    peers = diag_inverse.shape[1] // own
    core = lax.axis_index("core")
    y = lax.axis_index("y")
    left = jnp.concatenate([diag_inverse[0], diag_inverse[1]], axis=1)
    right = jnp.concatenate(
        [
            jnp.concatenate([panel_rhs[0], panel_rhs[1]], axis=1),
            jnp.concatenate([-panel_rhs[1], panel_rhs[0]], axis=1),
        ],
        axis=0,
    )
    partial = jnp.dot(left, right, precision=lax.Precision.HIGHEST, preferred_element_type=F32)
    earlier = jnp.einsum("sk,csm->ckm", modes_prev, solved_prev, preferred_element_type=F32)
    outgoing = jnp.concatenate(
        [
            partial[:, :width].reshape(peers, own, width),
            partial[:, width:].reshape(peers, own, width),
            earlier.reshape(peers, own, width),
        ],
        axis=1,
    )
    summed = jnp.sum(lax.all_to_all(outgoing, COL, 0, 0, tiled=True), axis=0)
    panel_solution = summed[: 2 * own].reshape(2, own, width)
    share = summed[2 * own :]
    high = lax.reduce_precision(share, 8, 7)
    low = share - high
    packed = jnp.concatenate(
        [summed[: 2 * own].astype(BF16), modes_panel, high.astype(BF16), low.astype(BF16)], axis=0
    )
    rows = packed.shape[0]
    gathered = lax.all_to_all(
        jnp.broadcast_to(packed[None], (peers, rows, width)), COL, 0, 0, tiled=True
    )
    block = (
        gathered[:, : 3 * own]
        .reshape(peers, 3, own, width)
        .transpose(1, 0, 2, 3)
        .reshape(3, peers * own, width)
    )
    share = gathered[:, 3 * own : 4 * own].astype(F32) + gathered[:, 4 * own :].astype(F32)
    share = share.reshape(2, width, width)
    mine = lax.dynamic_index_in_dim(share, core, 0, keepdims=False)
    other = lax.dynamic_index_in_dim(share, 1 - core, 0, keepdims=False)
    half = mine + lax.ppermute(other, "core", SWAP)
    blocks = jnp.stack([block] + [flipped(block, k) for k in (1, 2, 3)])
    half = (half + flipped(half, 2)) + (flipped(half, 1) + flipped(half, 3))
    ordered = jnp.stack(
        [lax.dynamic_index_in_dim(blocks, y ^ k, 0, keepdims=False) for k in range(4)]
    )
    solved = jnp.concatenate([ordered[:, 0], ordered[:, 1]], axis=2)
    theirs = lax.ppermute(solved, "core", SWAP)
    first = jnp.where(core == 0, solved, theirs)
    second = jnp.where(core == 0, theirs, solved)
    piece = jnp.stack([first, second], axis=1).reshape(-1, 2 * width)
    turned = jnp.concatenate([-piece[:, width:], piece[:, :width]], axis=1)
    update = jnp.dot(factor_slab[0], piece, preferred_element_type=F32) + jnp.dot(
        factor_slab[1], turned, preferred_element_type=F32
    )
    updated_rhs = jnp.stack(
        [pending_rhs[0] - update[:, :width], pending_rhs[1] - update[:, width:]]
    )
    latest = jnp.einsum(
        "ysk,cysm->ckm",
        ordered[:, 2],
        jnp.stack([ordered[:, 0], ordered[:, 1]]),
        preferred_element_type=F32,
    )
    both = jnp.stack([jnp.where(core == 0, half, 0.0), jnp.where(core == 1, half, 0.0)]) + latest
    modal_forces = both + lax.ppermute(both, "core", SWAP)
    return (panel_solution, updated_rhs, modal_forces)


def solution(mesh):
    fine = Mesh(mesh.devices.reshape(4, 2, 8, 4), ("y", "core", "z", "x"))
    row = ("y", "core")
    every = ("y", "core", "z", "x")
    placed = (
        P(None, row, COL),
        P(None, COL, None),
        P(None, every, None),
        P(None, every, None),
        P(None, every, None),
        P(every, None),
        P(every, None),
    )
    return jax.shard_map(
        on_device,
        mesh=fine,
        in_specs=placed,
        out_specs=(P(None, every, None), P(None, every, None), P()),
        check_vma=False,
    )
```

```python
import functools

import jax
import jax.numpy as jnp
from jax import lax
from jax.experimental import pallas as pl
from jax.experimental.pallas import tpu as pltpu
from jax.sharding import Mesh, PartitionSpec as P

F32 = jnp.float32
BF16 = jnp.bfloat16
COL = ("z", "x")
SWAP = [(0, 1), (1, 0)]
CHUNK = 128
TURNS = (0, 1, 3, 2)


def swapped(value):
    return lax.ppermute(value, "core", SWAP)


def flipped(value, bits):
    return lax.ppermute(value, "y", [(i, i ^ bits) for i in range(4)])


def first_kernel(diag_hbm, rhs_hbm, modes_hbm, solved_hbm, out_ref, diag_ref, rhs_ref, modes_ref, solved_ref, sems):
    peers, rows, width = out_ref.shape
    own = rows // 3
    moves = [
        pltpu.make_async_copy(source, target, sems.at[i])
        for i, (source, target) in enumerate(
            (
                (modes_hbm, modes_ref),
                (solved_hbm, solved_ref),
                (rhs_hbm, rhs_ref),
                (diag_hbm, diag_ref),
            )
        )
    ]
    for move in moves:
        move.start()
    over_first = (((0,), (0,)), ((), ()))
    half = peers // 2
    moves[0].wait()
    moves[1].wait()
    for c in range(2):
        earlier = lax.dot_general(
            modes_ref[...], solved_ref[c], over_first, preferred_element_type=F32
        )
        out_ref[c * half : (c + 1) * half, 2 * own :, :] = earlier.reshape(half, own, width)
    moves[2].wait()
    moves[3].wait()
    left = jnp.concatenate([diag_ref[0], diag_ref[1]], axis=0)
    real, imag = rhs_ref[0], rhs_ref[1]
    right = jnp.concatenate(
        [jnp.concatenate([real, imag], axis=1), jnp.concatenate([-imag, real], axis=1)], axis=0
    )
    partial = lax.dot_general(
        left, right, over_first, precision=lax.Precision.HIGHEST, preferred_element_type=F32
    )
    out_ref[:, :own, :] = partial[:, :width].reshape(peers, own, width)
    out_ref[:, own : 2 * own, :] = partial[:, width:].reshape(peers, own, width)


def first_partials(diag_inverse, panel_rhs, modes_prev, solved_prev, peers, own):
    width = panel_rhs.shape[2]
    args = (jnp.swapaxes(diag_inverse, 1, 2), panel_rhs, modes_prev, solved_prev)
    return pl.pallas_call(
        first_kernel,
        out_shape=jax.ShapeDtypeStruct((peers, 3 * own, width), F32),
        in_specs=[pl.BlockSpec(memory_space=pltpu.HBM)] * 4,
        out_specs=pl.BlockSpec(memory_space=pltpu.VMEM),
        scratch_shapes=[pltpu.VMEM(a.shape, a.dtype) for a in args]
        + [pltpu.SemaphoreType.DMA((4,))],
        name="partials",
    )(*args)


def update_kernel(turns, factor_ref, rhs_ref, *rest):
    out_ref = rest[-1]
    depth = rest[0].shape[0]
    rows = factor_ref.shape[1]
    width = out_ref.shape[2]
    y = lax.axis_index("y")
    core = lax.axis_index("core")
    for j, block_ref in enumerate(rest[:-1]):
        place = jnp.bitwise_xor(y, turns[j // 2]) * 2 + jnp.bitwise_xor(core, j % 2)
        columns = pl.ds(pl.multiple_of(place * depth, depth), depth)
        straight = block_ref[...]
        crossed = jnp.concatenate([-straight[:, width:], straight[:, :width]], axis=1)
        base = rhs_ref if j == 0 else out_ref
        for at in range(0, rows, CHUNK):
            span = slice(at, at + CHUNK)
            product = jnp.dot(factor_ref[0, span, columns], straight, preferred_element_type=F32)
            product += jnp.dot(factor_ref[1, span, columns], crossed, preferred_element_type=F32)
            out_ref[0, span, :] = base[0, span, :] - product[:, :width]
            out_ref[1, span, :] = base[1, span, :] - product[:, width:]


def update(turns, factor_slab, rhs, blocks, name):
    depth = blocks[0].shape[0]
    rows = factor_slab.shape[1]
    vmem = pl.BlockSpec(memory_space=pltpu.VMEM)
    return pl.pallas_call(
        functools.partial(update_kernel, turns),
        out_shape=jax.ShapeDtypeStruct(rhs.shape, F32),
        in_specs=[vmem] * (2 + len(blocks)),
        out_specs=vmem,
        cost_estimate=pl.CostEstimate(
            flops=len(blocks) * 4 * rows * depth * 2 * rhs.shape[2],
            bytes_accessed=len(blocks) * 4 * rows * depth,
            transcendentals=0,
        ),
        compiler_params=pltpu.CompilerParams(vmem_limit_bytes=24 << 20),
        name=name,
    )(factor_slab, rhs, *blocks)


def on_device(
    diag_inverse, panel_rhs, factor_slab, pending_rhs, solved_prev, modes_prev, modes_panel
):
    width = panel_rhs.shape[2]
    own = modes_panel.shape[0]
    peers = diag_inverse.shape[1] // own
    core = lax.axis_index("core")
    outgoing = first_partials(diag_inverse, panel_rhs, modes_prev, solved_prev, peers, own)
    summed = jnp.sum(lax.all_to_all(outgoing, COL, 0, 0, tiled=True), axis=0)
    panel_solution = summed[: 2 * own].reshape(2, own, width)
    share = summed[2 * own :]
    high = lax.reduce_precision(share, 8, 7)
    low = share - high
    packed = jnp.concatenate(
        [summed[: 2 * own].astype(BF16), modes_panel, high.astype(BF16), low.astype(BF16)], axis=0
    )
    rows = packed.shape[0]
    gathered = lax.all_to_all(
        jnp.broadcast_to(packed[None], (peers, rows, width)), COL, 0, 0, tiled=True
    )
    block = jnp.concatenate(
        [
            gathered[:, :own].reshape(peers * own, width),
            gathered[:, own : 2 * own].reshape(peers * own, width),
        ],
        axis=1,
    )
    beside = {k: flipped(block, k) for k in TURNS[1:]}
    twin = swapped(block)
    modes_block = gathered[:, 2 * own : 3 * own].reshape(peers * own, width)
    share = gathered[:, 3 * own : 4 * own].astype(F32) + gathered[:, 4 * own :].astype(F32)
    latest = lax.dot_general(
        modes_block, block, (((0,), (0,)), ((), ())), preferred_element_type=F32
    )
    share = share.reshape(2, width, width) + jnp.stack([latest[:, :width], latest[:, width:]])
    mine = lax.dynamic_index_in_dim(share, core, 0, keepdims=False)
    other = lax.dynamic_index_in_dim(share, 1 - core, 0, keepdims=False)
    half = mine + swapped(other)
    half, beside[1] = lax.optimization_barrier((half, beside[1]))
    half = (half + flipped(half, 2)) + (flipped(half, 1) + flipped(half, 3))
    back = swapped(half)
    started = update(TURNS[:1], factor_slab, pending_rhs, [block, twin], "update_own")
    twins = {k: swapped(beside[k]) for k in TURNS[1:]}
    updated_rhs = update(
        TURNS[1:],
        factor_slab,
        started,
        [b for k in TURNS[1:] for b in (beside[k], twins[k])],
        "update_rest",
    )
    modal_forces = jnp.stack(
        [jnp.where(core == 0, half, back), jnp.where(core == 0, back, half)]
    )
    return (panel_solution, updated_rhs, modal_forces)


def solution(mesh):
    fine = Mesh(mesh.devices.reshape(4, 2, 8, 4), ("y", "core", "z", "x"))
    row = ("y", "core")
    every = ("y", "core", "z", "x")
    placed = (
        P(None, row, COL),
        P(None, COL, None),
        P(None, every, None),
        P(None, every, None),
        P(None, every, None),
        P(every, None),
        P(every, None),
    )
    return jax.shard_map(
        on_device,
        mesh=fine,
        in_specs=placed,
        out_specs=(P(None, every, None), P(None, every, None), P()),
        check_vma=False,
    )
```

```python
import functools

import jax
import jax.numpy as jnp
from jax import lax
from jax.experimental import pallas as pl
from jax.experimental.pallas import tpu as pltpu
from jax.sharding import Mesh, PartitionSpec as P

F32 = jnp.float32
BF16 = jnp.bfloat16
COL = ("z", "x")
SWAP = [(0, 1), (1, 0)]
CHUNK = 128
TURNS = (0, 1, 3, 2)


def swapped(value):
    return lax.ppermute(value, "core", SWAP)


def flipped(value, bits):
    return lax.ppermute(value, "y", [(i, i ^ bits) for i in range(4)])


def first_kernel(diag_hbm, rhs_hbm, modes_hbm, solved_hbm, out_ref, diag_ref, rhs_ref, modes_ref, solved_ref, sems):
    peers, rows, width = out_ref.shape
    own = rows // 3
    moves = [
        pltpu.make_async_copy(source, target, sems.at[i])
        for i, (source, target) in enumerate(
            (
                (modes_hbm, modes_ref),
                (solved_hbm, solved_ref),
                (rhs_hbm, rhs_ref),
                (diag_hbm, diag_ref),
            )
        )
    ]
    for move in moves:
        move.start()
    over_first = (((0,), (0,)), ((), ()))
    half = peers // 2
    moves[0].wait()
    moves[1].wait()
    for c in range(2):
        earlier = lax.dot_general(
            modes_ref[...], solved_ref[c], over_first, preferred_element_type=F32
        )
        out_ref[c * half : (c + 1) * half, 2 * own :, :] = earlier.reshape(half, own, width)
    moves[2].wait()
    moves[3].wait()
    left = jnp.concatenate([diag_ref[0], diag_ref[1]], axis=0)
    real, imag = rhs_ref[0], rhs_ref[1]
    right = jnp.concatenate(
        [jnp.concatenate([real, imag], axis=1), jnp.concatenate([-imag, real], axis=1)], axis=0
    )
    partial = lax.dot_general(
        left, right, over_first, precision=lax.Precision.HIGHEST, preferred_element_type=F32
    )
    out_ref[:, :own, :] = partial[:, :width].reshape(peers, own, width)
    out_ref[:, own : 2 * own, :] = partial[:, width:].reshape(peers, own, width)


def first_partials(diag_inverse, panel_rhs, modes_prev, solved_prev, peers, own):
    width = panel_rhs.shape[2]
    args = (jnp.swapaxes(diag_inverse, 1, 2), panel_rhs, modes_prev, solved_prev)
    return pl.pallas_call(
        first_kernel,
        out_shape=jax.ShapeDtypeStruct((peers, 3 * own, width), F32),
        in_specs=[pl.BlockSpec(memory_space=pltpu.HBM)] * 4,
        out_specs=pl.BlockSpec(memory_space=pltpu.VMEM),
        scratch_shapes=[pltpu.VMEM(a.shape, a.dtype) for a in args]
        + [pltpu.SemaphoreType.DMA((4,))],
        name="partials",
    )(*args)


def update_kernel(turns, factor_ref, rhs_ref, *rest):
    out_ref = rest[-1]
    depth = rest[0].shape[0]
    rows = factor_ref.shape[1]
    width = out_ref.shape[2]
    y = lax.axis_index("y")
    core = lax.axis_index("core")
    for j, block_ref in enumerate(rest[:-1]):
        place = jnp.bitwise_xor(y, turns[j // 2]) * 2 + jnp.bitwise_xor(core, j % 2)
        columns = pl.ds(pl.multiple_of(place * depth, depth), depth)
        straight = block_ref[...]
        crossed = jnp.concatenate([-straight[:, width:], straight[:, :width]], axis=1)
        base = rhs_ref if j == 0 else out_ref
        for at in range(0, rows, CHUNK):
            span = slice(at, at + CHUNK)
            product = jnp.dot(factor_ref[0, span, columns], straight, preferred_element_type=F32)
            product += jnp.dot(factor_ref[1, span, columns], crossed, preferred_element_type=F32)
            out_ref[0, span, :] = base[0, span, :] - product[:, :width]
            out_ref[1, span, :] = base[1, span, :] - product[:, width:]


def update(turns, factor_slab, rhs, blocks, name):
    depth = blocks[0].shape[0]
    rows = factor_slab.shape[1]
    vmem = pl.BlockSpec(memory_space=pltpu.VMEM)
    return pl.pallas_call(
        functools.partial(update_kernel, turns),
        out_shape=jax.ShapeDtypeStruct(rhs.shape, F32),
        in_specs=[vmem] * (2 + len(blocks)),
        out_specs=vmem,
        cost_estimate=pl.CostEstimate(
            flops=len(blocks) * 4 * rows * depth * 2 * rhs.shape[2],
            bytes_accessed=len(blocks) * 4 * rows * depth,
            transcendentals=0,
        ),
        compiler_params=pltpu.CompilerParams(vmem_limit_bytes=24 << 20),
        name=name,
    )(factor_slab, rhs, *blocks)


def on_device(
    diag_inverse, panel_rhs, factor_slab, pending_rhs, solved_prev, modes_prev, modes_panel
):
    width = panel_rhs.shape[2]
    own = modes_panel.shape[0]
    peers = diag_inverse.shape[1] // own
    core = lax.axis_index("core")
    outgoing = first_partials(diag_inverse, panel_rhs, modes_prev, solved_prev, peers, own)
    summed = jnp.sum(lax.all_to_all(outgoing, COL, 0, 0, tiled=True), axis=0)
    panel_solution = summed[: 2 * own].reshape(2, own, width)
    share = summed[2 * own :]
    high = lax.reduce_precision(share, 8, 7)
    low = share - high
    packed = jnp.concatenate(
        [summed[: 2 * own].astype(BF16), modes_panel, high.astype(BF16), low.astype(BF16)], axis=0
    )
    rows = packed.shape[0]
    gathered = lax.all_to_all(
        jnp.broadcast_to(packed[None], (peers, rows, width)), COL, 0, 0, tiled=True
    )
    block = jnp.concatenate(
        [
            gathered[:, :own].reshape(peers * own, width),
            gathered[:, own : 2 * own].reshape(peers * own, width),
        ],
        axis=1,
    )
    beside = {k: flipped(block, k) for k in TURNS[1:]}
    twin = swapped(block)
    modes_block = gathered[:, 2 * own : 3 * own].reshape(peers * own, width)
    share = gathered[:, 3 * own : 4 * own].astype(F32) + gathered[:, 4 * own :].astype(F32)
    latest = lax.dot_general(
        modes_block, block, (((0,), (0,)), ((), ())), preferred_element_type=F32
    )
    share = share.reshape(2, width, width) + jnp.stack([latest[:, :width], latest[:, width:]])
    mine = lax.dynamic_index_in_dim(share, core, 0, keepdims=False)
    other = lax.dynamic_index_in_dim(share, 1 - core, 0, keepdims=False)
    half = mine + swapped(other)
    started = update(TURNS[:1], factor_slab, pending_rhs, [block, twin], "update_own")
    half, started, landed = lax.optimization_barrier(
        (half, started, [beside[k] for k in TURNS[1:]])
    )
    beside = dict(zip(TURNS[1:], landed))
    twins = {k: swapped(beside[k]) for k in TURNS[1:]}
    others = [flipped(half, k) for k in (1, 2, 3)]
    updated_rhs = update(
        TURNS[1:],
        factor_slab,
        started,
        [b for k in TURNS[1:] for b in (beside[k], twins[k])],
        "update_rest",
    )
    others, updated_rhs = lax.optimization_barrier((others, updated_rhs))
    half = (half + others[1]) + (others[0] + others[2])
    back = swapped(half)
    modal_forces = jnp.stack(
        [jnp.where(core == 0, half, back), jnp.where(core == 0, back, half)]
    )
    return (panel_solution, updated_rhs, modal_forces)


def solution(mesh):
    fine = Mesh(mesh.devices.reshape(4, 2, 8, 4), ("y", "core", "z", "x"))
    row = ("y", "core")
    every = ("y", "core", "z", "x")
    placed = (
        P(None, row, COL),
        P(None, COL, None),
        P(None, every, None),
        P(None, every, None),
        P(None, every, None),
        P(every, None),
        P(every, None),
    )
    return jax.shard_map(
        on_device,
        mesh=fine,
        in_specs=placed,
        out_specs=(P(None, every, None), P(None, every, None), P()),
        check_vma=False,
    )
```

```python
import functools

import jax
import jax.numpy as jnp
from jax import lax
from jax.experimental import pallas as pl
from jax.experimental.pallas import tpu as pltpu
from jax.sharding import Mesh, PartitionSpec as P

F32 = jnp.float32
BF16 = jnp.bfloat16
COL = ("z", "x")
SWAP = [(0, 1), (1, 0)]
CHUNK = 128
TURNS = (0, 1, 3, 2)


def swapped(value):
    return lax.ppermute(value, "core", SWAP)


def flipped(value, axis, bits):
    size = lax.axis_size(axis)
    return lax.ppermute(value, axis, [(i, i ^ bits) for i in range(size)])


def first_kernel(diag_hbm, rhs_hbm, modes_hbm, solved_hbm, out_ref, earlier_ref, diag_ref, rhs_ref, modes_ref, solved_ref, sems):
    peers, rows, width = out_ref.shape
    own = rows // 2
    moves = [
        pltpu.make_async_copy(source, target, sems.at[i])
        for i, (source, target) in enumerate(
            (
                (modes_hbm, modes_ref),
                (solved_hbm, solved_ref),
                (rhs_hbm, rhs_ref),
                (diag_hbm, diag_ref),
            )
        )
    ]
    for move in moves:
        move.start()
    over_first = (((0,), (0,)), ((), ()))
    moves[0].wait()
    moves[1].wait()
    for c in range(2):
        earlier_ref[c] = lax.dot_general(
            modes_ref[...], solved_ref[c], over_first, preferred_element_type=F32
        )
    moves[2].wait()
    moves[3].wait()
    left = jnp.concatenate([diag_ref[0], diag_ref[1]], axis=0)
    real, imag = rhs_ref[0], rhs_ref[1]
    right = jnp.concatenate(
        [jnp.concatenate([real, imag], axis=1), jnp.concatenate([-imag, real], axis=1)], axis=0
    )
    partial = lax.dot_general(
        left, right, over_first, precision=lax.Precision.HIGHEST, preferred_element_type=F32
    )
    out_ref[:, :own, :] = partial[:, :width].reshape(peers, own, width)
    out_ref[:, own:, :] = partial[:, width:].reshape(peers, own, width)


def first_partials(diag_inverse, panel_rhs, modes_prev, solved_prev, peers, own):
    width = panel_rhs.shape[2]
    args = (jnp.swapaxes(diag_inverse, 1, 2), panel_rhs, modes_prev, solved_prev)
    return pl.pallas_call(
        first_kernel,
        out_shape=(
            jax.ShapeDtypeStruct((peers, 2 * own, width), F32),
            jax.ShapeDtypeStruct((2, width, width), F32),
        ),
        in_specs=[pl.BlockSpec(memory_space=pltpu.HBM)] * 4,
        out_specs=(pl.BlockSpec(memory_space=pltpu.VMEM),) * 2,
        scratch_shapes=[pltpu.VMEM(a.shape, a.dtype) for a in args]
        + [pltpu.SemaphoreType.DMA((4,))],
        name="partials",
    )(*args)


def update_kernel(turns, factor_ref, rhs_ref, *rest):
    out_ref = rest[-1]
    depth = rest[0].shape[0]
    rows = factor_ref.shape[1]
    width = out_ref.shape[2]
    y = lax.axis_index("y")
    core = lax.axis_index("core")
    for j, block_ref in enumerate(rest[:-1]):
        place = jnp.bitwise_xor(y, turns[j // 2]) * 2 + jnp.bitwise_xor(core, j % 2)
        columns = pl.ds(pl.multiple_of(place * depth, depth), depth)
        straight = block_ref[...]
        crossed = jnp.concatenate([-straight[:, width:], straight[:, :width]], axis=1)
        base = rhs_ref if j == 0 else out_ref
        for at in range(0, rows, CHUNK):
            span = slice(at, at + CHUNK)
            product = jnp.dot(factor_ref[0, span, columns], straight, preferred_element_type=F32)
            product += jnp.dot(factor_ref[1, span, columns], crossed, preferred_element_type=F32)
            out_ref[0, span, :] = base[0, span, :] - product[:, :width]
            out_ref[1, span, :] = base[1, span, :] - product[:, width:]


def update(turns, factor_slab, rhs, blocks, name):
    depth = blocks[0].shape[0]
    rows = factor_slab.shape[1]
    vmem = pl.BlockSpec(memory_space=pltpu.VMEM)
    return pl.pallas_call(
        functools.partial(update_kernel, turns),
        out_shape=jax.ShapeDtypeStruct(rhs.shape, F32),
        in_specs=[vmem] * (2 + len(blocks)),
        out_specs=vmem,
        cost_estimate=pl.CostEstimate(
            flops=len(blocks) * 4 * rows * depth * 2 * rhs.shape[2],
            bytes_accessed=len(blocks) * 4 * rows * depth,
            transcendentals=0,
        ),
        compiler_params=pltpu.CompilerParams(vmem_limit_bytes=24 << 20),
        name=name,
    )(factor_slab, rhs, *blocks)


def split(value):
    high = lax.reduce_precision(value, 8, 7)
    return jnp.concatenate([high.astype(BF16), (value - high).astype(BF16)], axis=0)


def joined(pair):
    count = pair.shape[0] // 2
    return pair[:count].astype(F32) + pair[count:].astype(F32)


def once(step, carry):
    count = lax.optimization_barrier(jnp.int32(1))
    return lax.fori_loop(0, count, lambda _, held: step(held), carry)


def doubled(total, modes, axis, bit):
    count = 2 * total.shape[0]
    width = total.shape[1]
    mine = split(total)
    sent = jnp.concatenate([mine, modes.reshape(-1, width)], axis=0)
    came = flipped(sent, axis, bit)
    total = joined(mine) + joined(came[:count])
    theirs = came[count:].reshape(modes.shape)
    lower = (lax.axis_index(axis) & bit) == 0
    modes = jnp.stack([jnp.where(lower, modes, theirs), jnp.where(lower, theirs, modes)])
    return total, modes.reshape((-1,) + modes.shape[2:])


def on_device(
    diag_inverse, panel_rhs, factor_slab, pending_rhs, solved_prev, modes_prev, modes_panel
):
    width = panel_rhs.shape[2]
    own = modes_panel.shape[0]
    peers = diag_inverse.shape[1] // own
    core = lax.axis_index("core")
    y = lax.axis_index("y")
    outgoing, earlier = first_partials(
        diag_inverse, panel_rhs, modes_prev, solved_prev, peers, own
    )
    came = lax.all_to_all(outgoing, COL, 0, 0, tiled=True)

    def near(carry):
        earlier, total, modes = carry
        mine = lax.dynamic_index_in_dim(earlier, core, 0, keepdims=False)
        other = lax.dynamic_index_in_dim(earlier, 1 - core, 0, keepdims=False)
        half = (mine + swapped(other)).reshape(4, width // 4, width)
        total = lax.dynamic_index_in_dim(half, y, 0, keepdims=False)
        rows = [modes_panel]
        for k in (1, 2, 3):
            chunk = lax.dynamic_index_in_dim(half, y ^ k, 0, keepdims=False)
            part = flipped(jnp.concatenate([split(chunk), modes_panel], axis=0), "y", k)
            total = total + joined(part[: 2 * width // 4])
            rows.append(part[2 * width // 4 :])
        rows = jnp.stack(rows)[None]
        total, rows = doubled(total, rows, "x", 1)
        total, rows = doubled(total, rows, "x", 2)
        return earlier, total, rows

    total = jnp.zeros((width // 4, width), F32)
    modes = jnp.zeros((4, 4, own, width), BF16)
    earlier, total, modes = once(near, (earlier, total, modes))
    came, total, modes = lax.optimization_barrier((came, total, modes))

    panel_solution = jnp.sum(came, axis=0)
    rounded = panel_solution.astype(BF16)
    panel_solution = panel_solution.reshape(2, own, width)
    gathered = lax.all_to_all(
        jnp.broadcast_to(rounded[None], (peers, 2 * own, width)), COL, 0, 0, tiled=True
    )

    def far(carry):
        total, rows, _ = carry
        after, rows = doubled(total, rows, "z", 1)
        after, wide = doubled(after, rows, "z", 2)
        return total, carry[1], (after, wide)

    wide = (jnp.zeros_like(total), jnp.zeros((16, 4, own, width), BF16))
    _, _, (total, modes) = once(far, (total, modes, wide))
    gathered, total, modes = lax.optimization_barrier((gathered, total, modes))

    block = jnp.concatenate(
        [
            gathered[:, :own].reshape(peers * own, width),
            gathered[:, own:].reshape(peers * own, width),
        ],
        axis=1,
    )
    beside = [flipped(block, "y", k) for k in TURNS[1:]]
    twin = swapped(block)
    total, modes = doubled(total, modes, "z", 4)
    started = update(TURNS[:1], factor_slab, pending_rhs, [block, twin], "update_own")
    started, beside, total, modes = lax.optimization_barrier((started, beside, total, modes))

    totals = [total] + [flipped(total, "y", k) for k in (1, 2, 3)]
    blocks = dict(zip(TURNS, [block] + beside))
    twins = [swapped(b) for b in beside]
    latest = [
        lax.dot_general(
            modes[:, k].reshape(peers * own, width),
            blocks[k],
            (((0,), (0,)), ((), ())),
            preferred_element_type=F32,
        )
        for k in range(4)
    ]
    latest = (latest[0] + latest[2]) + (latest[1] + latest[3])
    updated_rhs = update(
        TURNS[1:],
        factor_slab,
        started,
        [b for two in zip(beside, twins) for b in two],
        "update_rest",
    )
    totals, updated_rhs = lax.optimization_barrier((jnp.stack(totals), updated_rhs))
    earlier = jnp.concatenate(
        [lax.dynamic_index_in_dim(totals, y ^ k, 0, keepdims=False) for k in range(4)], axis=0
    )
    both = jnp.stack(
        [
            latest[:, :width] + jnp.where(core == 0, earlier, 0.0),
            latest[:, width:] + jnp.where(core == 1, earlier, 0.0),
        ]
    )
    modal_forces = both + swapped(both)
    return (panel_solution, updated_rhs, modal_forces)


def solution(mesh):
    fine = Mesh(mesh.devices.reshape(4, 2, 8, 4), ("y", "core", "z", "x"))
    row = ("y", "core")
    every = ("y", "core", "z", "x")
    placed = (
        P(None, row, COL),
        P(None, COL, None),
        P(None, every, None),
        P(None, every, None),
        P(None, every, None),
        P(every, None),
        P(every, None),
    )
    return jax.shard_map(
        on_device,
        mesh=fine,
        in_specs=placed,
        out_specs=(P(None, every, None), P(None, every, None), P()),
        check_vma=False,
    )
```

```python
import functools

import jax
import jax.numpy as jnp
from jax import lax
from jax.experimental import pallas as pl
from jax.experimental.pallas import tpu as pltpu
from jax.sharding import Mesh, PartitionSpec as P

F32 = jnp.float32
BF16 = jnp.bfloat16
COL = ("z", "x")
SWAP = [(0, 1), (1, 0)]
CHUNK = 128
TURNS = (0, 1, 3, 2)


def swapped(value):
    return lax.ppermute(value, "core", SWAP)


def flipped(value, bits):
    return lax.ppermute(value, "y", [(i, i ^ bits) for i in range(4)])


def split(value):
    high = lax.reduce_precision(value, 8, 7)
    return jnp.concatenate([high.astype(BF16), (value - high).astype(BF16)], axis=1)


def joined(pair):
    width = pair.shape[1] // 2
    return pair[:, :width].astype(F32) + pair[:, width:].astype(F32)


def first_kernel(diag_hbm, rhs_hbm, modes_hbm, solved_hbm, out_ref, diag_ref, rhs_ref, modes_ref, solved_ref, sems):
    peers, rows, width = out_ref.shape
    own = rows // 3
    moves = [
        pltpu.make_async_copy(source, target, sems.at[i])
        for i, (source, target) in enumerate(
            (
                (modes_hbm, modes_ref),
                (solved_hbm, solved_ref),
                (rhs_hbm, rhs_ref),
                (diag_hbm, diag_ref),
            )
        )
    ]
    for move in moves:
        move.start()
    over_first = (((0,), (0,)), ((), ()))
    half = peers // 2
    moves[0].wait()
    moves[1].wait()
    for c in range(2):
        earlier = lax.dot_general(
            modes_ref[...], solved_ref[c], over_first, preferred_element_type=F32
        )
        out_ref[c * half : (c + 1) * half, 2 * own :, :] = earlier.reshape(half, own, width)
    moves[2].wait()
    moves[3].wait()
    left = jnp.concatenate([diag_ref[0], diag_ref[1]], axis=0)
    real, imag = rhs_ref[0], rhs_ref[1]
    right = jnp.concatenate(
        [jnp.concatenate([real, imag], axis=1), jnp.concatenate([-imag, real], axis=1)], axis=0
    )
    partial = lax.dot_general(
        left, right, over_first, precision=lax.Precision.HIGHEST, preferred_element_type=F32
    )
    out_ref[:, :own, :] = partial[:, :width].reshape(peers, own, width)
    out_ref[:, own : 2 * own, :] = partial[:, width:].reshape(peers, own, width)


def first_partials(diag_inverse, panel_rhs, modes_prev, solved_prev, peers, own):
    width = panel_rhs.shape[2]
    args = (jnp.swapaxes(diag_inverse, 1, 2), panel_rhs, modes_prev, solved_prev)
    return pl.pallas_call(
        first_kernel,
        out_shape=jax.ShapeDtypeStruct((peers, 3 * own, width), F32),
        in_specs=[pl.BlockSpec(memory_space=pltpu.HBM)] * 4,
        out_specs=pl.BlockSpec(memory_space=pltpu.VMEM),
        scratch_shapes=[pltpu.VMEM(a.shape, a.dtype) for a in args]
        + [pltpu.SemaphoreType.DMA((4,))],
        name="partials",
    )(*args)


def update_kernel(turns, factor_ref, rhs_ref, *rest):
    out_ref = rest[-1]
    width = out_ref.shape[2]
    depth = 2 * width
    rows = factor_ref.shape[1]
    y = lax.axis_index("y")
    core = lax.axis_index("core")
    for j, block_ref in enumerate(rest[:-1]):
        place = jnp.bitwise_xor(y, turns[j // 2]) * 2 + jnp.bitwise_xor(core, j % 2)
        columns = pl.ds(pl.multiple_of(place * depth, depth), depth)
        straight = block_ref[:depth, :]
        crossed = jnp.concatenate([-straight[:, width:], straight[:, :width]], axis=1)
        base = rhs_ref if j == 0 else out_ref
        for at in range(0, rows, CHUNK):
            span = slice(at, at + CHUNK)
            product = jnp.dot(factor_ref[0, span, columns], straight, preferred_element_type=F32)
            product += jnp.dot(factor_ref[1, span, columns], crossed, preferred_element_type=F32)
            out_ref[0, span, :] = base[0, span, :] - product[:, :width]
            out_ref[1, span, :] = base[1, span, :] - product[:, width:]


def update(turns, factor_slab, rhs, blocks, name):
    depth = 2 * rhs.shape[2]
    rows = factor_slab.shape[1]
    vmem = pl.BlockSpec(memory_space=pltpu.VMEM)
    return pl.pallas_call(
        functools.partial(update_kernel, turns),
        out_shape=jax.ShapeDtypeStruct(rhs.shape, F32),
        in_specs=[vmem] * (2 + len(blocks)),
        out_specs=vmem,
        cost_estimate=pl.CostEstimate(
            flops=len(blocks) * 4 * rows * depth * 2 * rhs.shape[2],
            bytes_accessed=len(blocks) * 4 * rows * depth,
            transcendentals=0,
        ),
        compiler_params=pltpu.CompilerParams(vmem_limit_bytes=24 << 20),
        name=name,
    )(factor_slab, rhs, *blocks)


def on_device(
    diag_inverse, panel_rhs, factor_slab, pending_rhs, solved_prev, modes_prev, modes_panel
):
    width = panel_rhs.shape[2]
    own = modes_panel.shape[0]
    peers = diag_inverse.shape[1] // own
    core = lax.axis_index("core")
    outgoing = first_partials(diag_inverse, panel_rhs, modes_prev, solved_prev, peers, own)
    summed = jnp.sum(lax.all_to_all(outgoing, COL, 0, 0, tiled=True), axis=0)
    panel_solution = summed[: 2 * own].reshape(2, own, width)
    share = summed[2 * own :]
    high = lax.reduce_precision(share, 8, 7)
    low = share - high
    packed = jnp.concatenate(
        [summed[: 2 * own].astype(BF16), modes_panel, high.astype(BF16), low.astype(BF16)], axis=0
    )
    rows = packed.shape[0]
    gathered = lax.all_to_all(
        jnp.broadcast_to(packed[None], (peers, rows, width)), COL, 0, 0, tiled=True
    )
    block = jnp.concatenate(
        [
            gathered[:, :own].reshape(peers * own, width),
            gathered[:, own : 2 * own].reshape(peers * own, width),
        ],
        axis=1,
    )
    twin = swapped(block)
    modes_block = gathered[:, 2 * own : 3 * own].reshape(peers * own, width)
    share = gathered[:, 3 * own : 4 * own].astype(F32) + gathered[:, 4 * own :].astype(F32)
    latest = lax.dot_general(
        modes_block, block, (((0,), (0,)), ((), ())), preferred_element_type=F32
    )
    share = share.reshape(2, width, width) + jnp.stack([latest[:, :width], latest[:, width:]])
    mine = lax.dynamic_index_in_dim(share, core, 0, keepdims=False)
    other = lax.dynamic_index_in_dim(share, 1 - core, 0, keepdims=False)
    half = split(mine + swapped(other))
    sent = jnp.concatenate([block, half], axis=0)
    came = [flipped(sent, k) for k in TURNS[1:]]
    started = update(TURNS[:1], factor_slab, pending_rhs, [block, twin], "update_own")
    started, came = lax.optimization_barrier((started, came))
    depth = block.shape[0]
    twins = [swapped(c[:depth]) for c in came]
    first, third, second = (joined(c[depth:]) for c in came)
    half = (joined(half) + second) + (first + third)
    back = swapped(half)
    updated_rhs = update(
        TURNS[1:],
        factor_slab,
        started,
        [b for two in zip(came, twins) for b in two],
        "update_rest",
    )
    modal_forces = jnp.stack(
        [jnp.where(core == 0, half, back), jnp.where(core == 0, back, half)]
    )
    return (panel_solution, updated_rhs, modal_forces)


def solution(mesh):
    fine = Mesh(mesh.devices.reshape(4, 2, 8, 4), ("y", "core", "z", "x"))
    row = ("y", "core")
    every = ("y", "core", "z", "x")
    placed = (
        P(None, row, COL),
        P(None, COL, None),
        P(None, every, None),
        P(None, every, None),
        P(None, every, None),
        P(every, None),
        P(every, None),
    )
    return jax.shard_map(
        on_device,
        mesh=fine,
        in_specs=placed,
        out_specs=(P(None, every, None), P(None, every, None), P()),
        check_vma=False,
    )
```

```python
import functools

import jax
import jax.numpy as jnp
from jax import lax
from jax.experimental import pallas as pl
from jax.experimental.pallas import tpu as pltpu
from jax.sharding import Mesh, PartitionSpec as P

F32 = jnp.float32
BF16 = jnp.bfloat16
COL = ("z", "x")
SWAP = [(0, 1), (1, 0)]
CHUNK = 128
GRANT = 50 << 20
PACK_FLOPS = 1_000_000
TURNS = (0, 1, 3, 2)


def swapped(value):
    return lax.ppermute(value, "core", SWAP)


def flipped(value, bits):
    return lax.ppermute(value, "y", [(i, i ^ bits) for i in range(4)])


def split(value):
    high = lax.reduce_precision(value, 8, 7)
    return jnp.concatenate([high.astype(BF16), (value - high).astype(BF16)], axis=1)


def joined(pair):
    width = pair.shape[1] // 2
    return pair[:, :width].astype(F32) + pair[:, width:].astype(F32)


def first_kernel(diag_hbm, rhs_hbm, modes_hbm, solved_hbm, out_ref, diag_ref, rhs_ref, modes_ref, solved_ref, sems):
    peers, rows, width = out_ref.shape
    own = rows // 3
    moves = [
        pltpu.make_async_copy(source, target, sems.at[i])
        for i, (source, target) in enumerate(
            (
                (modes_hbm, modes_ref),
                (solved_hbm, solved_ref),
                (rhs_hbm, rhs_ref),
                (diag_hbm, diag_ref),
            )
        )
    ]
    for move in moves:
        move.start()
    over_first = (((0,), (0,)), ((), ()))
    half = peers // 2
    moves[0].wait()
    moves[1].wait()
    for c in range(2):
        earlier = lax.dot_general(
            modes_ref[...], solved_ref[c], over_first, preferred_element_type=F32
        )
        out_ref[c * half : (c + 1) * half, 2 * own :, :] = earlier.reshape(half, own, width)
    moves[2].wait()
    moves[3].wait()
    left = jnp.concatenate([diag_ref[0], diag_ref[1]], axis=0)
    real, imag = rhs_ref[0], rhs_ref[1]
    right = jnp.concatenate(
        [jnp.concatenate([real, imag], axis=1), jnp.concatenate([-imag, real], axis=1)], axis=0
    )
    partial = lax.dot_general(
        left, right, over_first, precision=lax.Precision.HIGHEST, preferred_element_type=F32
    )
    out_ref[:, :own, :] = partial[:, :width].reshape(peers, own, width)
    out_ref[:, own : 2 * own, :] = partial[:, width:].reshape(peers, own, width)


def first_partials(diag_inverse, panel_rhs, modes_prev, solved_prev, peers, own):
    width = panel_rhs.shape[2]
    args = (jnp.swapaxes(diag_inverse, 1, 2), panel_rhs, modes_prev, solved_prev)
    return pl.pallas_call(
        first_kernel,
        out_shape=jax.ShapeDtypeStruct((peers, 3 * own, width), F32),
        in_specs=[pl.BlockSpec(memory_space=pltpu.HBM)] * 4,
        out_specs=pl.BlockSpec(memory_space=pltpu.VMEM),
        scratch_shapes=[pltpu.VMEM(a.shape, a.dtype) for a in args]
        + [pltpu.SemaphoreType.DMA((4,))],
        name="partials",
    )(*args)


def pack_kernel(came_ref, modes_ref, panel_ref, packed_ref):
    own = modes_ref.shape[0]
    summed = jnp.sum(came_ref[...], axis=0)
    panel_ref[0] = summed[:own]
    panel_ref[1] = summed[own : 2 * own]
    share = summed[2 * own :]
    high = share.astype(BF16).astype(F32)
    rows = jnp.concatenate(
        [summed[: 2 * own], modes_ref[...].astype(F32), high, share - high], axis=0
    )
    packed_ref[...] = jnp.broadcast_to(rows.astype(BF16)[None], packed_ref.shape)


def pack(came, modes_panel):
    peers, rows, width = came.shape
    own = rows // 3
    vmem = pl.BlockSpec(memory_space=pltpu.VMEM)
    return pl.pallas_call(
        pack_kernel,
        out_shape=(
            jax.ShapeDtypeStruct((2, own, width), F32),
            jax.ShapeDtypeStruct((peers, 5 * own, width), BF16),
        ),
        in_specs=[vmem] * 2,
        out_specs=(vmem, vmem),
        cost_estimate=pl.CostEstimate(
            flops=PACK_FLOPS, bytes_accessed=came.size * 4, transcendentals=0
        ),
        compiler_params=pltpu.CompilerParams(vmem_limit_bytes=24 << 20),
        name="pack",
    )(came, modes_panel)


def update_kernel(turns, factor_hbm, rhs_ref, *rest):
    count = 2 * len(turns)
    blocks, (out_ref, held, sems) = rest[:count], rest[count:]
    width = out_ref.shape[2]
    depth = 2 * width
    rows = held.shape[2]
    y = lax.axis_index("y")
    core = lax.axis_index("core")
    moves = []
    for j in range(count):
        place = jnp.bitwise_xor(y, turns[j // 2]) * 2 + jnp.bitwise_xor(core, j % 2)
        columns = pl.ds(pl.multiple_of(place * depth, depth), depth)
        for c in range(2):
            moves.append(
                pltpu.make_async_copy(
                    factor_hbm.at[c, :, columns], held.at[j, c], sems.at[j, c]
                )
            )
    for move in moves:
        move.start()
    for j, block_ref in enumerate(blocks):
        straight = block_ref[:depth, :]
        crossed = jnp.concatenate([-straight[:, width:], straight[:, :width]], axis=1)
        base = rhs_ref if j == 0 else out_ref
        moves[2 * j].wait()
        moves[2 * j + 1].wait()
        for at in range(0, rows, CHUNK):
            span = slice(at, at + CHUNK)
            product = jnp.dot(held[j, 0, span, :], straight, preferred_element_type=F32)
            product += jnp.dot(held[j, 1, span, :], crossed, preferred_element_type=F32)
            out_ref[0, span, :] = base[0, span, :] - product[:, :width]
            out_ref[1, span, :] = base[1, span, :] - product[:, width:]


def update(turns, factor_slab, rhs, blocks, name):
    depth = 2 * rhs.shape[2]
    rows = factor_slab.shape[1]
    count = len(blocks)
    vmem = pl.BlockSpec(memory_space=pltpu.VMEM)
    return pl.pallas_call(
        functools.partial(update_kernel, turns),
        out_shape=jax.ShapeDtypeStruct(rhs.shape, F32),
        in_specs=[pl.BlockSpec(memory_space=pl.ANY)] + [vmem] * (1 + count),
        out_specs=vmem,
        scratch_shapes=[
            pltpu.VMEM((count, 2, rows, depth), BF16),
            pltpu.SemaphoreType.DMA((count, 2)),
        ],
        cost_estimate=pl.CostEstimate(
            flops=count * 4 * rows * depth * 2 * rhs.shape[2],
            bytes_accessed=count * 4 * rows * depth,
            transcendentals=0,
        ),
        compiler_params=pltpu.CompilerParams(vmem_limit_bytes=GRANT),
        name=name,
    )(factor_slab, rhs, *blocks)


def on_device(
    diag_inverse, panel_rhs, factor_slab, pending_rhs, solved_prev, modes_prev, modes_panel
):
    width = panel_rhs.shape[2]
    own = modes_panel.shape[0]
    peers = diag_inverse.shape[1] // own
    core = lax.axis_index("core")
    outgoing = first_partials(diag_inverse, panel_rhs, modes_prev, solved_prev, peers, own)
    came = lax.all_to_all(outgoing, COL, 0, 0, tiled=True)
    panel_solution, packed = pack(came, modes_panel)
    gathered = lax.all_to_all(packed, COL, 0, 0, tiled=True)
    block = jnp.concatenate(
        [
            gathered[:, :own].reshape(peers * own, width),
            gathered[:, own : 2 * own].reshape(peers * own, width),
        ],
        axis=1,
    )
    twin = swapped(block)
    modes_block = gathered[:, 2 * own : 3 * own].reshape(peers * own, width)
    share = gathered[:, 3 * own : 4 * own].astype(F32) + gathered[:, 4 * own :].astype(F32)
    latest = lax.dot_general(
        modes_block, block, (((0,), (0,)), ((), ())), preferred_element_type=F32
    )
    share = share.reshape(2, width, width) + jnp.stack([latest[:, :width], latest[:, width:]])
    mine = lax.dynamic_index_in_dim(share, core, 0, keepdims=False)
    other = lax.dynamic_index_in_dim(share, 1 - core, 0, keepdims=False)
    half = split(mine + swapped(other))
    sent = jnp.concatenate([block, half], axis=0)
    came = [flipped(sent, k) for k in TURNS[1:]]
    started = update(TURNS[:1], factor_slab, pending_rhs, [block, twin], "update_own")
    started, came = lax.optimization_barrier((started, came))
    depth = block.shape[0]
    twins = [swapped(c[:depth]) for c in came]
    first, third, second = (joined(c[depth:]) for c in came)
    half = (joined(half) + second) + (first + third)
    back = swapped(half)
    updated_rhs = update(
        TURNS[1:],
        factor_slab,
        started,
        [b for two in zip(came, twins) for b in two],
        "update_rest",
    )
    modal_forces = jnp.stack(
        [jnp.where(core == 0, half, back), jnp.where(core == 0, back, half)]
    )
    return (panel_solution, updated_rhs, modal_forces)


def solution(mesh):
    fine = Mesh(mesh.devices.reshape(4, 2, 8, 4), ("y", "core", "z", "x"))
    row = ("y", "core")
    every = ("y", "core", "z", "x")
    placed = (
        P(None, row, COL),
        P(None, COL, None),
        P(None, every, None),
        P(None, every, None),
        P(None, every, None),
        P(every, None),
        P(every, None),
    )
    return jax.shard_map(
        on_device,
        mesh=fine,
        in_specs=placed,
        out_specs=(P(None, every, None), P(None, every, None), P()),
        check_vma=False,
    )
```

```python
import functools

import jax
import jax.numpy as jnp
from jax import lax
from jax.experimental import pallas as pl
from jax.experimental.pallas import tpu as pltpu
from jax.sharding import Mesh, PartitionSpec as P

F32 = jnp.float32
BF16 = jnp.bfloat16
COL = ("z", "x")
SWAP = [(0, 1), (1, 0)]
CHUNK = 128
TURNS = (0, 1, 3, 2)


def swapped(value):
    return lax.ppermute(value, "core", SWAP)


def flipped(value, bits):
    return lax.ppermute(value, "y", [(i, i ^ bits) for i in range(4)])


def split(value):
    high = lax.reduce_precision(value, 8, 7)
    return jnp.concatenate([high.astype(BF16), (value - high).astype(BF16)], axis=1)


def joined(pair):
    width = pair.shape[1] // 2
    return pair[:, :width].astype(F32) + pair[:, width:].astype(F32)


def first_kernel(diag_hbm, rhs_hbm, modes_hbm, solved_hbm, out_ref, diag_ref, rhs_ref, modes_ref, solved_ref, sems):
    peers, rows, width = out_ref.shape
    own = rows // 3
    moves = [
        pltpu.make_async_copy(source, target, sems.at[i])
        for i, (source, target) in enumerate(
            (
                (modes_hbm, modes_ref),
                (solved_hbm, solved_ref),
                (rhs_hbm, rhs_ref),
                (diag_hbm, diag_ref),
            )
        )
    ]
    for move in moves:
        move.start()
    over_first = (((0,), (0,)), ((), ()))
    half = peers // 2
    moves[0].wait()
    moves[1].wait()
    for c in range(2):
        earlier = lax.dot_general(
            modes_ref[...], solved_ref[c], over_first, preferred_element_type=F32
        )
        out_ref[c * half : (c + 1) * half, 2 * own :, :] = earlier.reshape(half, own, width)
    moves[2].wait()
    moves[3].wait()
    left = jnp.concatenate([diag_ref[0], diag_ref[1]], axis=0)
    real, imag = rhs_ref[0], rhs_ref[1]
    right = jnp.concatenate(
        [jnp.concatenate([real, imag], axis=1), jnp.concatenate([-imag, real], axis=1)], axis=0
    )
    partial = lax.dot_general(
        left, right, over_first, precision=lax.Precision.HIGHEST, preferred_element_type=F32
    )
    out_ref[:, :own, :] = partial[:, :width].reshape(peers, own, width)
    out_ref[:, own : 2 * own, :] = partial[:, width:].reshape(peers, own, width)


def first_partials(diag_inverse, panel_rhs, modes_prev, solved_prev, peers, own):
    width = panel_rhs.shape[2]
    args = (jnp.swapaxes(diag_inverse, 1, 2), panel_rhs, modes_prev, solved_prev)
    return pl.pallas_call(
        first_kernel,
        out_shape=jax.ShapeDtypeStruct((peers, 3 * own, width), F32),
        in_specs=[pl.BlockSpec(memory_space=pltpu.HBM)] * 4,
        out_specs=pl.BlockSpec(memory_space=pltpu.VMEM),
        scratch_shapes=[pltpu.VMEM(a.shape, a.dtype) for a in args]
        + [pltpu.SemaphoreType.DMA((4,))],
        name="partials",
    )(*args)


def pack_kernel(came_ref, modes_ref, panel_ref, packed_ref):
    own = modes_ref.shape[0]
    summed = jnp.sum(came_ref[...], axis=0)
    panel_ref[...] = summed
    share = summed[2 * own :]
    high = share.astype(BF16).astype(F32)
    rows = jnp.concatenate(
        [summed[: 2 * own], modes_ref[...], high, share - high], axis=0
    )
    packed_ref[...] = jnp.broadcast_to(rows.astype(BF16)[None], packed_ref.shape)


def pack(came, modes_panel):
    peers, rows, width = came.shape
    own = rows // 3
    vmem = pl.BlockSpec(memory_space=pltpu.VMEM)
    return pl.pallas_call(
        pack_kernel,
        out_shape=(
            jax.ShapeDtypeStruct((3 * own, width), F32),
            jax.ShapeDtypeStruct((peers, 5 * own, width), BF16),
        ),
        in_specs=[vmem] * 2,
        out_specs=(vmem, vmem),
        cost_estimate=pl.CostEstimate(
            flops=came.size, bytes_accessed=came.size * 4, transcendentals=0
        ),
        compiler_params=pltpu.CompilerParams(vmem_limit_bytes=24 << 20),
        name="pack",
    )(came, modes_panel)


def update_kernel(turns, factor_ref, rhs_ref, *rest):
    out_ref = rest[-1]
    width = out_ref.shape[2]
    depth = 2 * width
    rows = factor_ref.shape[1]
    y = lax.axis_index("y")
    core = lax.axis_index("core")
    for j, block_ref in enumerate(rest[:-1]):
        place = jnp.bitwise_xor(y, turns[j // 2]) * 2 + jnp.bitwise_xor(core, j % 2)
        columns = pl.ds(pl.multiple_of(place * depth, depth), depth)
        straight = block_ref[:depth, :]
        crossed = jnp.concatenate([-straight[:, width:], straight[:, :width]], axis=1)
        base = rhs_ref if j == 0 else out_ref
        for at in range(0, rows, CHUNK):
            span = slice(at, at + CHUNK)
            product = jnp.dot(factor_ref[0, span, columns], straight, preferred_element_type=F32)
            product += jnp.dot(factor_ref[1, span, columns], crossed, preferred_element_type=F32)
            out_ref[0, span, :] = base[0, span, :] - product[:, :width]
            out_ref[1, span, :] = base[1, span, :] - product[:, width:]


def update(turns, factor_slab, rhs, blocks, name):
    depth = 2 * rhs.shape[2]
    rows = factor_slab.shape[1]
    vmem = pl.BlockSpec(memory_space=pltpu.VMEM)
    return pl.pallas_call(
        functools.partial(update_kernel, turns),
        out_shape=jax.ShapeDtypeStruct(rhs.shape, F32),
        in_specs=[vmem] * (2 + len(blocks)),
        out_specs=vmem,
        cost_estimate=pl.CostEstimate(
            flops=len(blocks) * 4 * rows * depth * 2 * rhs.shape[2],
            bytes_accessed=len(blocks) * 4 * rows * depth,
            transcendentals=0,
        ),
        compiler_params=pltpu.CompilerParams(vmem_limit_bytes=24 << 20),
        name=name,
    )(factor_slab, rhs, *blocks)


def on_device(
    diag_inverse, panel_rhs, factor_slab, pending_rhs, solved_prev, modes_prev, modes_panel
):
    width = panel_rhs.shape[2]
    own = modes_panel.shape[0]
    peers = diag_inverse.shape[1] // own
    outgoing = first_partials(diag_inverse, panel_rhs, modes_prev, solved_prev, peers, own)
    came = lax.all_to_all(outgoing, COL, 0, 0, tiled=True)
    panel_solution, packed = pack(came, modes_panel.astype(F32))
    panel_solution = panel_solution[: 2 * own].reshape(2, own, width)
    gathered = lax.all_to_all(packed, COL, 0, 0, tiled=True)
    block = jnp.concatenate(
        [
            gathered[:, :own].reshape(peers * own, width),
            gathered[:, own : 2 * own].reshape(peers * own, width),
        ],
        axis=1,
    )
    twin = swapped(block)
    modes_block = gathered[:, 2 * own : 3 * own].reshape(peers * own, width)
    share = gathered[:, 3 * own : 4 * own].astype(F32) + gathered[:, 4 * own :].astype(F32)
    latest = lax.dot_general(
        modes_block, block, (((0,), (0,)), ((), ())), preferred_element_type=F32
    )
    share = share.reshape(2, width, width) + jnp.stack([latest[:, :width], latest[:, width:]])
    modal = split(share.reshape(2 * width, width))
    sent = jnp.concatenate([block, modal], axis=0)
    came = [flipped(sent, k) for k in TURNS[1:]]
    started = update(TURNS[:1], factor_slab, pending_rhs, [block, twin], "update_own")
    started, came = lax.optimization_barrier((started, came))
    depth = block.shape[0]
    twins = [swapped(c[:depth]) for c in came]
    first, third, second = (joined(c[depth:]) for c in came)
    modal = (joined(modal) + second) + (first + third)
    modal_forces = (modal + swapped(modal)).reshape(2, width, width)
    updated_rhs = update(
        TURNS[1:],
        factor_slab,
        started,
        [b for two in zip(came, twins) for b in two],
        "update_rest",
    )
    return (panel_solution, updated_rhs, modal_forces)


def solution(mesh):
    fine = Mesh(mesh.devices.reshape(4, 2, 8, 4), ("y", "core", "z", "x"))
    row = ("y", "core")
    every = ("y", "core", "z", "x")
    placed = (
        P(None, row, COL),
        P(None, COL, None),
        P(None, every, None),
        P(None, every, None),
        P(None, every, None),
        P(every, None),
        P(every, None),
    )
    return jax.shard_map(
        on_device,
        mesh=fine,
        in_specs=placed,
        out_specs=(P(None, every, None), P(None, every, None), P()),
        check_vma=False,
    )
```

```python
import functools

import jax
import jax.numpy as jnp
from jax import lax
from jax.experimental import pallas as pl
from jax.experimental.pallas import tpu as pltpu
from jax.sharding import Mesh, PartitionSpec as P

F32 = jnp.float32
BF16 = jnp.bfloat16
COL = ("z", "x")
SWAP = [(0, 1), (1, 0)]
CHUNK = 128
TURNS = ((0, 0), (1, 3), (3, 1), (2, 2))


def swapped(value):
    return lax.ppermute(value, "core", SWAP)


def flipped(value, turn):
    pairs = [(2 * y + core, 2 * (y ^ turn[core]) + core) for y in range(4) for core in range(2)]
    return lax.ppermute(value, ("y", "core"), pairs)


def split(value):
    high = lax.reduce_precision(value, 8, 7)
    return jnp.concatenate([high.astype(BF16), (value - high).astype(BF16)], axis=1)


def joined(pair):
    width = pair.shape[1] // 2
    return pair[:, :width].astype(F32) + pair[:, width:].astype(F32)


def first_kernel(diag_hbm, rhs_hbm, modes_hbm, solved_hbm, out_ref, diag_ref, rhs_ref, modes_ref, solved_ref, sems):
    peers, rows, width = out_ref.shape
    own = rows // 3
    moves = [
        pltpu.make_async_copy(source, target, sems.at[i])
        for i, (source, target) in enumerate(
            (
                (modes_hbm, modes_ref),
                (solved_hbm, solved_ref),
                (rhs_hbm, rhs_ref),
                (diag_hbm, diag_ref),
            )
        )
    ]
    for move in moves:
        move.start()
    over_first = (((0,), (0,)), ((), ()))
    half = peers // 2
    moves[0].wait()
    moves[1].wait()
    for c in range(2):
        earlier = lax.dot_general(
            modes_ref[...], solved_ref[c], over_first, preferred_element_type=F32
        )
        out_ref[c * half : (c + 1) * half, 2 * own :, :] = earlier.reshape(half, own, width)
    moves[2].wait()
    moves[3].wait()
    left = jnp.concatenate([diag_ref[0], diag_ref[1]], axis=0)
    real, imag = rhs_ref[0], rhs_ref[1]
    right = jnp.concatenate(
        [jnp.concatenate([real, imag], axis=1), jnp.concatenate([-imag, real], axis=1)], axis=0
    )
    partial = lax.dot_general(
        left, right, over_first, precision=lax.Precision.HIGHEST, preferred_element_type=F32
    )
    out_ref[:, :own, :] = partial[:, :width].reshape(peers, own, width)
    out_ref[:, own : 2 * own, :] = partial[:, width:].reshape(peers, own, width)


def first_partials(diag_inverse, panel_rhs, modes_prev, solved_prev, peers, own):
    width = panel_rhs.shape[2]
    args = (jnp.swapaxes(diag_inverse, 1, 2), panel_rhs, modes_prev, solved_prev)
    return pl.pallas_call(
        first_kernel,
        out_shape=jax.ShapeDtypeStruct((peers, 3 * own, width), F32),
        in_specs=[pl.BlockSpec(memory_space=pltpu.HBM)] * 4,
        out_specs=pl.BlockSpec(memory_space=pltpu.VMEM),
        scratch_shapes=[pltpu.VMEM(a.shape, a.dtype) for a in args]
        + [pltpu.SemaphoreType.DMA((4,))],
        name="partials",
    )(*args)


def pack_kernel(came_ref, modes_ref, panel_ref, packed_ref):
    own = modes_ref.shape[0]
    summed = jnp.sum(came_ref[...], axis=0)
    panel_ref[...] = summed
    share = summed[2 * own :]
    high = share.astype(BF16).astype(F32)
    rows = jnp.concatenate(
        [summed[: 2 * own], modes_ref[...], high, share - high], axis=0
    )
    packed_ref[...] = jnp.broadcast_to(rows.astype(BF16)[None], packed_ref.shape)


def pack(came, modes_panel):
    peers, rows, width = came.shape
    own = rows // 3
    vmem = pl.BlockSpec(memory_space=pltpu.VMEM)
    return pl.pallas_call(
        pack_kernel,
        out_shape=(
            jax.ShapeDtypeStruct((3 * own, width), F32),
            jax.ShapeDtypeStruct((peers, 5 * own, width), BF16),
        ),
        in_specs=[vmem] * 2,
        out_specs=(vmem, vmem),
        cost_estimate=pl.CostEstimate(
            flops=came.size, bytes_accessed=came.size * 4, transcendentals=0
        ),
        compiler_params=pltpu.CompilerParams(vmem_limit_bytes=24 << 20),
        name="pack",
    )(came, modes_panel)


def update_kernel(turns, factor_ref, rhs_ref, *rest):
    count = 2 * len(turns)
    blocks, rest = rest[:count], rest[count:]
    if len(rest) == 1:
        (out_ref,) = rest
    else:
        modal_ref, back_ref, summed_ref, out_ref, forces_ref, panel_ref = rest
        forces_ref[...] = modal_ref[...] + back_ref[...]
        panel_ref[...] = summed_ref[: panel_ref.shape[0], :]
    width = out_ref.shape[2]
    depth = 2 * width
    rows = factor_ref.shape[1]
    y = lax.axis_index("y")
    core = lax.axis_index("core")
    pieces = []
    for j, block_ref in enumerate(blocks):
        source = core if j % 2 == 0 else 1 - core
        low, high = turns[j // 2]
        place = jnp.bitwise_xor(y, low + (high - low) * source) * 2 + source
        columns = pl.ds(pl.multiple_of(place * depth, depth), depth)
        straight = block_ref[:depth, :]
        crossed = jnp.concatenate([-straight[:, width:], straight[:, :width]], axis=1)
        pieces.append((columns, straight, crossed))
    for at in range(0, rows, CHUNK):
        span = slice(at, at + CHUNK)
        product = jnp.zeros((CHUNK, depth), F32)
        for columns, straight, crossed in pieces:
            product += jnp.dot(factor_ref[0, span, columns], straight, preferred_element_type=F32)
            product += jnp.dot(factor_ref[1, span, columns], crossed, preferred_element_type=F32)
        out_ref[0, span, :] = rhs_ref[0, span, :] - product[:, :width]
        out_ref[1, span, :] = rhs_ref[1, span, :] - product[:, width:]


def update(turns, factor_slab, rhs, blocks, name, others=()):
    depth = 2 * rhs.shape[2]
    rows = factor_slab.shape[1]
    vmem = pl.BlockSpec(memory_space=pltpu.VMEM)
    shapes = [jax.ShapeDtypeStruct(rhs.shape, F32)]
    if others:
        modal, _, summed = others
        shapes.append(jax.ShapeDtypeStruct(modal.shape, F32))
        shapes.append(jax.ShapeDtypeStruct((summed.shape[0] * 2 // 3, summed.shape[1]), F32))
    return pl.pallas_call(
        functools.partial(update_kernel, turns),
        out_shape=shapes,
        in_specs=[vmem] * (2 + len(blocks) + len(others)),
        out_specs=[vmem] * len(shapes),
        cost_estimate=pl.CostEstimate(
            flops=len(blocks) * 4 * rows * depth * 2 * rhs.shape[2],
            bytes_accessed=len(blocks) * 4 * rows * depth,
            transcendentals=0,
        ),
        compiler_params=pltpu.CompilerParams(vmem_limit_bytes=24 << 20),
        name=name,
    )(factor_slab, rhs, *blocks, *others)


def on_device(
    diag_inverse, panel_rhs, factor_slab, pending_rhs, solved_prev, modes_prev, modes_panel
):
    width = panel_rhs.shape[2]
    own = modes_panel.shape[0]
    peers = diag_inverse.shape[1] // own
    outgoing = first_partials(diag_inverse, panel_rhs, modes_prev, solved_prev, peers, own)
    came = lax.all_to_all(outgoing, COL, 0, 0, tiled=True)
    summed, packed = pack(came, modes_panel.astype(F32))
    gathered = lax.all_to_all(packed, COL, 0, 0, tiled=True)
    block = jnp.concatenate(
        [
            gathered[:, :own].reshape(peers * own, width),
            gathered[:, own : 2 * own].reshape(peers * own, width),
        ],
        axis=1,
    )
    twin = swapped(block)
    modes_block = gathered[:, 2 * own : 3 * own].reshape(peers * own, width)
    share = gathered[:, 3 * own : 4 * own].astype(F32) + gathered[:, 4 * own :].astype(F32)
    latest = lax.dot_general(
        modes_block, block, (((0,), (0,)), ((), ())), preferred_element_type=F32
    )
    share = share.reshape(2, width, width) + jnp.stack([latest[:, :width], latest[:, width:]])
    modal = split(share.reshape(2 * width, width))
    sent = jnp.concatenate([block, modal], axis=0)
    came = [flipped(sent, k) for k in TURNS[1:]]
    (started,) = update(TURNS[:1], factor_slab, pending_rhs, [block, twin], "update_own")
    started, came = lax.optimization_barrier((started, came))
    depth = block.shape[0]
    twins = [swapped(c[:depth]) for c in came]
    first, third, second = (joined(c[depth:]) for c in came)
    modal = (joined(modal) + second) + (first + third)
    updated_rhs, modal_forces, panel_solution = update(
        TURNS[1:],
        factor_slab,
        started,
        [b for two in zip(came, twins) for b in two],
        "update_rest",
        (modal, swapped(modal), summed),
    )
    modal_forces = modal_forces.reshape(2, width, width)
    panel_solution = panel_solution.reshape(2, own, width)
    return (panel_solution, updated_rhs, modal_forces)


def solution(mesh):
    fine = Mesh(mesh.devices.reshape(4, 2, 8, 4), ("y", "core", "z", "x"))
    row = ("y", "core")
    every = ("y", "core", "z", "x")
    placed = (
        P(None, row, COL),
        P(None, COL, None),
        P(None, every, None),
        P(None, every, None),
        P(None, every, None),
        P(every, None),
        P(every, None),
    )
    return jax.shard_map(
        on_device,
        mesh=fine,
        in_specs=placed,
        out_specs=(P(None, every, None), P(None, every, None), P()),
        check_vma=False,
    )
```

```python
import functools

import jax
import jax.numpy as jnp
from jax import lax
from jax.experimental import pallas as pl
from jax.experimental.pallas import tpu as pltpu
from jax.sharding import Mesh, PartitionSpec as P

F32 = jnp.float32
BF16 = jnp.bfloat16
COL = ("z", "x")
SWAP = [(0, 1), (1, 0)]
CHUNK = 128
OWN = ((0, 0),)
EARLY = ((2, 2),)
LATE = ((1, 3), (3, 1))


def swapped(value):
    return lax.ppermute(value, "core", SWAP)


def flipped(value, turn):
    pairs = [(2 * y + core, 2 * (y ^ turn[core]) + core) for y in range(4) for core in range(2)]
    return lax.ppermute(value, ("y", "core"), pairs)


def split(value):
    high = lax.reduce_precision(value, 8, 7)
    return jnp.concatenate([high.astype(BF16), (value - high).astype(BF16)], axis=1)


def joined(pair):
    width = pair.shape[1] // 2
    return pair[:, :width].astype(F32) + pair[:, width:].astype(F32)


def first_kernel(diag_hbm, rhs_hbm, modes_hbm, solved_hbm, out_ref, diag_ref, rhs_ref, modes_ref, solved_ref, sems):
    peers, rows, width = out_ref.shape
    own = rows // 3
    moves = [
        pltpu.make_async_copy(source, target, sems.at[i])
        for i, (source, target) in enumerate(
            (
                (modes_hbm, modes_ref),
                (solved_hbm, solved_ref),
                (rhs_hbm, rhs_ref),
                (diag_hbm, diag_ref),
            )
        )
    ]
    for move in moves:
        move.start()
    over_first = (((0,), (0,)), ((), ()))
    half = peers // 2
    moves[0].wait()
    moves[1].wait()
    for c in range(2):
        earlier = lax.dot_general(
            modes_ref[...], solved_ref[c], over_first, preferred_element_type=F32
        )
        out_ref[c * half : (c + 1) * half, 2 * own :, :] = earlier.reshape(half, own, width)
    moves[2].wait()
    moves[3].wait()
    left = jnp.concatenate([diag_ref[0], diag_ref[1]], axis=0)
    real, imag = rhs_ref[0], rhs_ref[1]
    right = jnp.concatenate(
        [jnp.concatenate([real, imag], axis=1), jnp.concatenate([-imag, real], axis=1)], axis=0
    )
    partial = lax.dot_general(
        left, right, over_first, precision=lax.Precision.HIGHEST, preferred_element_type=F32
    )
    out_ref[:, :own, :] = partial[:, :width].reshape(peers, own, width)
    out_ref[:, own : 2 * own, :] = partial[:, width:].reshape(peers, own, width)


def first_partials(diag_inverse, panel_rhs, modes_prev, solved_prev, peers, own):
    width = panel_rhs.shape[2]
    args = (jnp.swapaxes(diag_inverse, 1, 2), panel_rhs, modes_prev, solved_prev)
    return pl.pallas_call(
        first_kernel,
        out_shape=jax.ShapeDtypeStruct((peers, 3 * own, width), F32),
        in_specs=[pl.BlockSpec(memory_space=pltpu.HBM)] * 4,
        out_specs=pl.BlockSpec(memory_space=pltpu.VMEM),
        scratch_shapes=[pltpu.VMEM(a.shape, a.dtype) for a in args]
        + [pltpu.SemaphoreType.DMA((4,))],
        name="partials",
    )(*args)


def pack_kernel(came_ref, modes_ref, panel_ref, packed_ref):
    own = modes_ref.shape[0]
    summed = jnp.sum(came_ref[...], axis=0)
    panel_ref[...] = summed
    share = summed[2 * own :]
    high = share.astype(BF16).astype(F32)
    rows = jnp.concatenate(
        [summed[: 2 * own], modes_ref[...], high, share - high], axis=0
    )
    packed_ref[...] = jnp.broadcast_to(rows.astype(BF16)[None], packed_ref.shape)


def pack(came, modes_panel):
    peers, rows, width = came.shape
    own = rows // 3
    vmem = pl.BlockSpec(memory_space=pltpu.VMEM)
    return pl.pallas_call(
        pack_kernel,
        out_shape=(
            jax.ShapeDtypeStruct((3 * own, width), F32),
            jax.ShapeDtypeStruct((peers, 5 * own, width), BF16),
        ),
        in_specs=[vmem] * 2,
        out_specs=(vmem, vmem),
        cost_estimate=pl.CostEstimate(
            flops=came.size, bytes_accessed=came.size * 4, transcendentals=0
        ),
        compiler_params=pltpu.CompilerParams(vmem_limit_bytes=24 << 20),
        name="pack",
    )(came, modes_panel)


def update_kernel(turns, factor_ref, rhs_ref, *rest):
    count = 2 * len(turns)
    blocks, rest = rest[:count], rest[count:]
    if len(rest) == 1:
        (out_ref,) = rest
    else:
        modal_ref, back_ref, summed_ref, out_ref, forces_ref, panel_ref = rest
        forces_ref[...] = modal_ref[...] + back_ref[...]
        panel_ref[...] = summed_ref[: panel_ref.shape[0], :]
    width = out_ref.shape[2]
    depth = 2 * width
    rows = factor_ref.shape[1]
    y = lax.axis_index("y")
    core = lax.axis_index("core")
    pieces = []
    for j, block_ref in enumerate(blocks):
        source = core if j % 2 == 0 else 1 - core
        low, high = turns[j // 2]
        place = jnp.bitwise_xor(y, low + (high - low) * source) * 2 + source
        columns = pl.ds(pl.multiple_of(place * depth, depth), depth)
        straight = block_ref[:depth, :]
        crossed = jnp.concatenate([-straight[:, width:], straight[:, :width]], axis=1)
        pieces.append((columns, straight, crossed))
    for at in range(0, rows, CHUNK):
        span = slice(at, at + CHUNK)
        product = jnp.zeros((CHUNK, depth), F32)
        for columns, straight, crossed in pieces:
            product += jnp.dot(factor_ref[0, span, columns], straight, preferred_element_type=F32)
            product += jnp.dot(factor_ref[1, span, columns], crossed, preferred_element_type=F32)
        out_ref[0, span, :] = rhs_ref[0, span, :] - product[:, :width]
        out_ref[1, span, :] = rhs_ref[1, span, :] - product[:, width:]


def update(turns, factor_slab, rhs, blocks, name, others=()):
    depth = 2 * rhs.shape[2]
    rows = factor_slab.shape[1]
    vmem = pl.BlockSpec(memory_space=pltpu.VMEM)
    shapes = [jax.ShapeDtypeStruct(rhs.shape, F32)]
    if others:
        modal, _, summed = others
        shapes.append(jax.ShapeDtypeStruct(modal.shape, F32))
        shapes.append(jax.ShapeDtypeStruct((summed.shape[0] * 2 // 3, summed.shape[1]), F32))
    return pl.pallas_call(
        functools.partial(update_kernel, turns),
        out_shape=shapes,
        in_specs=[vmem] * (2 + len(blocks) + len(others)),
        out_specs=[vmem] * len(shapes),
        cost_estimate=pl.CostEstimate(
            flops=len(blocks) * 4 * rows * depth * 2 * rhs.shape[2],
            bytes_accessed=len(blocks) * 4 * rows * depth,
            transcendentals=0,
        ),
        compiler_params=pltpu.CompilerParams(vmem_limit_bytes=24 << 20),
        name=name,
    )(factor_slab, rhs, *blocks, *others)


def on_device(
    diag_inverse, panel_rhs, factor_slab, pending_rhs, solved_prev, modes_prev, modes_panel
):
    width = panel_rhs.shape[2]
    own = modes_panel.shape[0]
    peers = diag_inverse.shape[1] // own
    outgoing = first_partials(diag_inverse, panel_rhs, modes_prev, solved_prev, peers, own)
    came = lax.all_to_all(outgoing, COL, 0, 0, tiled=True)
    summed, packed = pack(came, modes_panel.astype(F32))
    gathered = lax.all_to_all(packed, COL, 0, 0, tiled=True)
    block = jnp.concatenate(
        [
            gathered[:, :own].reshape(peers * own, width),
            gathered[:, own : 2 * own].reshape(peers * own, width),
        ],
        axis=1,
    )
    twin = swapped(block)
    modes_block = gathered[:, 2 * own : 3 * own].reshape(peers * own, width)
    share = gathered[:, 3 * own : 4 * own].astype(F32) + gathered[:, 4 * own :].astype(F32)
    latest = lax.dot_general(
        modes_block, block, (((0,), (0,)), ((), ())), preferred_element_type=F32
    )
    share = share.reshape(2, width, width) + jnp.stack([latest[:, :width], latest[:, width:]])
    modal = split(share.reshape(2 * width, width))
    sent = jnp.concatenate([block, modal], axis=0)
    head = flipped(sent, EARLY[0])
    tail = [flipped(sent, turn) for turn in LATE]
    depth = block.shape[0]
    (started,) = update(OWN, factor_slab, pending_rhs, [block, twin], "update_own")
    started, head = lax.optimization_barrier((started, head))
    (started,) = update(
        EARLY, factor_slab, started, [head, swapped(head[:depth])], "update_early"
    )
    started, tail = lax.optimization_barrier((started, tail))
    twins = [swapped(c[:depth]) for c in tail]
    first, third, second = (joined(c[depth:]) for c in (*tail, head))
    modal = (joined(modal) + second) + (first + third)
    updated_rhs, modal_forces, panel_solution = update(
        LATE,
        factor_slab,
        started,
        [b for two in zip(tail, twins) for b in two],
        "update_late",
        (modal, swapped(modal), summed),
    )
    modal_forces = modal_forces.reshape(2, width, width)
    panel_solution = panel_solution.reshape(2, own, width)
    return (panel_solution, updated_rhs, modal_forces)


def solution(mesh):
    fine = Mesh(mesh.devices.reshape(4, 2, 8, 4), ("y", "core", "z", "x"))
    row = ("y", "core")
    every = ("y", "core", "z", "x")
    placed = (
        P(None, row, COL),
        P(None, COL, None),
        P(None, every, None),
        P(None, every, None),
        P(None, every, None),
        P(every, None),
        P(every, None),
    )
    return jax.shard_map(
        on_device,
        mesh=fine,
        in_specs=placed,
        out_specs=(P(None, every, None), P(None, every, None), P()),
        check_vma=False,
    )
```

```python
import jax
import jax.numpy as jnp
from jax import lax
from jax.experimental import pallas as pl
from jax.experimental.pallas import tpu as pltpu
from jax.sharding import Mesh, PartitionSpec as P

F32 = jnp.float32
BF16 = jnp.bfloat16
COL = ("z", "x")
SWAP = [(0, 1), (1, 0)]
CHUNK = 128
TURNS = ((0, 0), (1, 3), (3, 1), (2, 2))


def swapped(value):
    return lax.ppermute(value, "core", SWAP)


def flipped(value, turn):
    pairs = [(2 * y + core, 2 * (y ^ turn[core]) + core) for y in range(4) for core in range(2)]
    return lax.ppermute(value, ("y", "core"), pairs)


def split(value):
    high = lax.reduce_precision(value, 8, 7)
    return jnp.concatenate([high.astype(BF16), (value - high).astype(BF16)], axis=1)


def joined(pair):
    width = pair.shape[1] // 2
    return pair[:, :width].astype(F32) + pair[:, width:].astype(F32)


def first_kernel(diag_hbm, rhs_hbm, modes_hbm, solved_hbm, out_ref, diag_ref, rhs_ref, modes_ref, solved_ref, sems):
    peers, rows, width = out_ref.shape
    own = rows // 3
    moves = [
        pltpu.make_async_copy(source, target, sems.at[i])
        for i, (source, target) in enumerate(
            (
                (modes_hbm, modes_ref),
                (solved_hbm, solved_ref),
                (rhs_hbm, rhs_ref),
                (diag_hbm, diag_ref),
            )
        )
    ]
    for move in moves:
        move.start()
    over_first = (((0,), (0,)), ((), ()))
    half = peers // 2
    moves[0].wait()
    moves[1].wait()
    for c in range(2):
        earlier = lax.dot_general(
            modes_ref[...], solved_ref[c], over_first, preferred_element_type=F32
        )
        out_ref[c * half : (c + 1) * half, 2 * own :, :] = earlier.reshape(half, own, width)
    moves[2].wait()
    moves[3].wait()
    left = jnp.concatenate([diag_ref[0], diag_ref[1]], axis=0)
    real, imag = rhs_ref[0], rhs_ref[1]
    right = jnp.concatenate(
        [jnp.concatenate([real, imag], axis=1), jnp.concatenate([-imag, real], axis=1)], axis=0
    )
    partial = lax.dot_general(
        left, right, over_first, precision=lax.Precision.HIGHEST, preferred_element_type=F32
    )
    out_ref[:, :own, :] = partial[:, :width].reshape(peers, own, width)
    out_ref[:, own : 2 * own, :] = partial[:, width:].reshape(peers, own, width)


def first_partials(diag_inverse, panel_rhs, modes_prev, solved_prev, peers, own):
    width = panel_rhs.shape[2]
    args = (jnp.swapaxes(diag_inverse, 1, 2), panel_rhs, modes_prev, solved_prev)
    return pl.pallas_call(
        first_kernel,
        out_shape=jax.ShapeDtypeStruct((peers, 3 * own, width), F32),
        in_specs=[pl.BlockSpec(memory_space=pltpu.HBM)] * 4,
        out_specs=pl.BlockSpec(memory_space=pltpu.VMEM),
        scratch_shapes=[pltpu.VMEM(a.shape, a.dtype) for a in args]
        + [pltpu.SemaphoreType.DMA((4,))],
        name="partials",
    )(*args)


def pack_kernel(came_ref, modes_ref, panel_ref, packed_ref):
    own = modes_ref.shape[0]
    summed = jnp.sum(came_ref[...], axis=0)
    panel_ref[...] = summed
    share = summed[2 * own :]
    high = share.astype(BF16).astype(F32)
    rows = jnp.concatenate(
        [summed[: 2 * own], modes_ref[...], high, share - high], axis=0
    )
    packed_ref[...] = jnp.broadcast_to(rows.astype(BF16)[None], packed_ref.shape)


def pack(came, modes_panel):
    peers, rows, width = came.shape
    own = rows // 3
    vmem = pl.BlockSpec(memory_space=pltpu.VMEM)
    return pl.pallas_call(
        pack_kernel,
        out_shape=(
            jax.ShapeDtypeStruct((3 * own, width), F32),
            jax.ShapeDtypeStruct((peers, 5 * own, width), BF16),
        ),
        in_specs=[vmem] * 2,
        out_specs=(vmem, vmem),
        cost_estimate=pl.CostEstimate(
            flops=came.size, bytes_accessed=came.size * 4, transcendentals=0
        ),
        compiler_params=pltpu.CompilerParams(vmem_limit_bytes=24 << 20),
        name="pack",
    )(came, modes_panel)


def block_pieces(turns, blocks, depth):
    y = lax.axis_index("y")
    core = lax.axis_index("core")
    pieces = []
    for j, block_ref in enumerate(blocks):
        source = core if j % 2 == 0 else 1 - core
        low, high = turns[j // 2]
        place = jnp.bitwise_xor(y, low + (high - low) * source) * 2 + source
        columns = pl.ds(pl.multiple_of(place * depth, depth), depth)
        straight = block_ref[:depth, :]
        half = depth // 2
        crossed = jnp.concatenate([-straight[:, half:], straight[:, :half]], axis=1)
        pieces.append((columns, straight, crossed))
    return pieces


def subtract(factor_ref, rhs_ref, out_ref, pieces, span):
    width = out_ref.shape[2]
    product = jnp.zeros((CHUNK, 2 * width), F32)
    for columns, straight, crossed in pieces:
        product += jnp.dot(factor_ref[0, span, columns], straight, preferred_element_type=F32)
        product += jnp.dot(factor_ref[1, span, columns], crossed, preferred_element_type=F32)
    out_ref[0, span, :] = rhs_ref[0, span, :] - product[:, :width]
    out_ref[1, span, :] = rhs_ref[1, span, :] - product[:, width:]


def own_kernel(factor_ref, rhs_ref, block_ref, twin_ref, out_ref):
    pieces = block_pieces(TURNS[:1], (block_ref, twin_ref), 2 * out_ref.shape[2])
    for at in range(0, out_ref.shape[1], CHUNK):
        subtract(factor_ref, rhs_ref, out_ref, pieces, slice(at, at + CHUNK))


def update_own(factor_slab, rhs, block, twin):
    vmem = pl.BlockSpec(memory_space=pltpu.VMEM)
    return pl.pallas_call(
        own_kernel,
        out_shape=jax.ShapeDtypeStruct(rhs.shape, F32),
        in_specs=[vmem] * 4,
        out_specs=vmem,
        cost_estimate=update_cost(factor_slab, rhs, 2),
        compiler_params=pltpu.CompilerParams(vmem_limit_bytes=24 << 20),
        name="update_own",
    )(factor_slab, rhs, block, twin)


def rest_kernel(factor_ref, rhs_ref, pair_ref, summed_ref, *rest):
    count = 2 * len(TURNS[1:])
    blocks = rest[:count]
    out_hbm, forces_hbm, panel_hbm, out_ref, forces_ref, panel_ref, sems = rest[count:]
    depth = 2 * out_ref.shape[2]
    forces_ref[...] = joined(pair_ref[...]) + joined(blocks[-1][depth:, :])
    panel_ref[...] = summed_ref[: panel_ref.shape[0], :]
    moves = [
        pltpu.make_async_copy(forces_ref, forces_hbm, sems.at[0]),
        pltpu.make_async_copy(panel_ref, panel_hbm, sems.at[1]),
    ]
    for move in moves:
        move.start()
    pieces = block_pieces(TURNS[1:], blocks, depth)
    for at in range(0, out_ref.shape[1], CHUNK):
        subtract(factor_ref, rhs_ref, out_ref, pieces, slice(at, at + CHUNK))
        rows = pl.ds(at, CHUNK)
        move = pltpu.make_async_copy(
            out_ref.at[:, rows, :], out_hbm.at[:, rows, :], sems.at[2 + at // CHUNK]
        )
        move.start()
        moves.append(move)
    for move in moves:
        move.wait()


def update_rest(factor_slab, rhs, blocks, pair, summed):
    width = rhs.shape[2]
    vmem = pl.BlockSpec(memory_space=pltpu.VMEM)
    shapes = [rhs.shape, (pair.shape[0], width), (summed.shape[0] * 2 // 3, width)]
    return pl.pallas_call(
        rest_kernel,
        out_shape=[jax.ShapeDtypeStruct(shape, F32) for shape in shapes],
        in_specs=[vmem] * (4 + len(blocks)),
        out_specs=[pl.BlockSpec(memory_space=pl.ANY)] * len(shapes),
        scratch_shapes=[pltpu.VMEM(shape, F32) for shape in shapes]
        + [pltpu.SemaphoreType.DMA((2 + rhs.shape[1] // CHUNK,))],
        cost_estimate=update_cost(factor_slab, rhs, len(blocks)),
        compiler_params=pltpu.CompilerParams(vmem_limit_bytes=24 << 20),
        name="update_rest",
    )(factor_slab, rhs, pair, summed, *blocks)


def update_cost(factor_slab, rhs, count):
    elements = count * 2 * factor_slab.shape[1] * 2 * rhs.shape[2]
    return pl.CostEstimate(
        flops=elements * 4 * rhs.shape[2], bytes_accessed=2 * elements, transcendentals=0
    )


def on_device(
    diag_inverse, panel_rhs, factor_slab, pending_rhs, solved_prev, modes_prev, modes_panel
):
    width = panel_rhs.shape[2]
    own = modes_panel.shape[0]
    peers = diag_inverse.shape[1] // own
    outgoing = first_partials(diag_inverse, panel_rhs, modes_prev, solved_prev, peers, own)
    came = lax.all_to_all(outgoing, COL, 0, 0, tiled=True)
    summed, packed = pack(came, modes_panel.astype(F32))
    gathered = lax.all_to_all(packed, COL, 0, 0, tiled=True)
    block = jnp.concatenate(
        [
            gathered[:, :own].reshape(peers * own, width),
            gathered[:, own : 2 * own].reshape(peers * own, width),
        ],
        axis=1,
    )
    twin = swapped(block)
    modes_block = gathered[:, 2 * own : 3 * own].reshape(peers * own, width)
    share = gathered[:, 3 * own : 4 * own].astype(F32) + gathered[:, 4 * own :].astype(F32)
    latest = lax.dot_general(
        modes_block, block, (((0,), (0,)), ((), ())), preferred_element_type=F32
    )
    share = share.reshape(2, width, width) + jnp.stack([latest[:, :width], latest[:, width:]])
    modal = split(share.reshape(2 * width, width))
    sent = jnp.concatenate([block, modal], axis=0)
    came = [flipped(sent, k) for k in TURNS[1:]]
    started = update_own(factor_slab, pending_rhs, block, twin)
    started, came = lax.optimization_barrier((started, came))
    depth = block.shape[0]
    first, third, second = (joined(c[depth:]) for c in came)
    pair = split((joined(modal) + second) + (first + third))
    twins = [swapped(c[:depth]) for c in came[:-1]]
    twins.append(swapped(jnp.concatenate([came[-1][:depth], pair], axis=0)))
    updated_rhs, modal_forces, panel_solution = update_rest(
        factor_slab, started, [b for two in zip(came, twins) for b in two], pair, summed
    )
    modal_forces = modal_forces.reshape(2, width, width)
    panel_solution = panel_solution.reshape(2, own, width)
    return (panel_solution, updated_rhs, modal_forces)


def solution(mesh):
    fine = Mesh(mesh.devices.reshape(4, 2, 8, 4), ("y", "core", "z", "x"))
    row = ("y", "core")
    every = ("y", "core", "z", "x")
    placed = (
        P(None, row, COL),
        P(None, COL, None),
        P(None, every, None),
        P(None, every, None),
        P(None, every, None),
        P(every, None),
        P(every, None),
    )
    return jax.shard_map(
        on_device,
        mesh=fine,
        in_specs=placed,
        out_specs=(P(None, every, None), P(None, every, None), P()),
        check_vma=False,
    )
```

```python
import functools

import jax
import jax.numpy as jnp
from jax import lax
from jax.experimental import pallas as pl
from jax.experimental.pallas import tpu as pltpu
from jax.sharding import Mesh, PartitionSpec as P

F32 = jnp.float32
BF16 = jnp.bfloat16
COL = ("z", "x")
SWAP = [(0, 1), (1, 0)]
CHUNK = 128
OWN = ((0, 0),)
EARLY = ((2, 2),)
LATE = ((1, 3), (3, 1))


def swapped(value):
    return lax.ppermute(value, "core", SWAP)


def flipped(value, turn):
    pairs = [(2 * y + core, 2 * (y ^ turn[core]) + core) for y in range(4) for core in range(2)]
    return lax.ppermute(value, ("y", "core"), pairs)


def split(value):
    high = lax.reduce_precision(value, 8, 7)
    return jnp.concatenate([high.astype(BF16), (value - high).astype(BF16)], axis=1)


def joined(pair):
    width = pair.shape[1] // 2
    return pair[:, :width].astype(F32) + pair[:, width:].astype(F32)


def first_kernel(diag_hbm, rhs_hbm, modes_hbm, solved_hbm, out_ref, diag_ref, rhs_ref, modes_ref, solved_ref, sems):
    peers, rows, width = out_ref.shape
    own = rows // 3
    moves = [
        pltpu.make_async_copy(source, target, sems.at[i])
        for i, (source, target) in enumerate(
            (
                (modes_hbm, modes_ref),
                (solved_hbm, solved_ref),
                (rhs_hbm, rhs_ref),
                (diag_hbm, diag_ref),
            )
        )
    ]
    for move in moves:
        move.start()
    over_first = (((0,), (0,)), ((), ()))
    half = peers // 2
    moves[0].wait()
    moves[1].wait()
    for c in range(2):
        earlier = lax.dot_general(
            modes_ref[...], solved_ref[c], over_first, preferred_element_type=F32
        )
        out_ref[c * half : (c + 1) * half, 2 * own :, :] = earlier.reshape(half, own, width)
    moves[2].wait()
    moves[3].wait()
    left = jnp.concatenate([diag_ref[0], diag_ref[1]], axis=0)
    real, imag = rhs_ref[0], rhs_ref[1]
    right = jnp.concatenate(
        [jnp.concatenate([real, imag], axis=1), jnp.concatenate([-imag, real], axis=1)], axis=0
    )
    partial = lax.dot_general(
        left, right, over_first, precision=lax.Precision.HIGHEST, preferred_element_type=F32
    )
    out_ref[:, :own, :] = partial[:, :width].reshape(peers, own, width)
    out_ref[:, own : 2 * own, :] = partial[:, width:].reshape(peers, own, width)


def first_partials(diag_inverse, panel_rhs, modes_prev, solved_prev, peers, own):
    width = panel_rhs.shape[2]
    args = (jnp.swapaxes(diag_inverse, 1, 2), panel_rhs, modes_prev, solved_prev)
    return pl.pallas_call(
        first_kernel,
        out_shape=jax.ShapeDtypeStruct((peers, 3 * own, width), F32),
        in_specs=[pl.BlockSpec(memory_space=pltpu.HBM)] * 4,
        out_specs=pl.BlockSpec(memory_space=pltpu.VMEM),
        scratch_shapes=[pltpu.VMEM(a.shape, a.dtype) for a in args]
        + [pltpu.SemaphoreType.DMA((4,))],
        name="partials",
    )(*args)


def pack_kernel(came_ref, modes_ref, panel_ref, packed_ref):
    own = modes_ref.shape[0]
    summed = jnp.sum(came_ref[...], axis=0)
    panel_ref[...] = summed
    share = summed[2 * own :]
    high = share.astype(BF16).astype(F32)
    rows = jnp.concatenate(
        [summed[: 2 * own], modes_ref[...], high, share - high], axis=0
    )
    packed_ref[...] = jnp.broadcast_to(rows.astype(BF16)[None], packed_ref.shape)


def pack(came, modes_panel):
    peers, rows, width = came.shape
    own = rows // 3
    vmem = pl.BlockSpec(memory_space=pltpu.VMEM)
    return pl.pallas_call(
        pack_kernel,
        out_shape=(
            jax.ShapeDtypeStruct((3 * own, width), F32),
            jax.ShapeDtypeStruct((peers, 5 * own, width), BF16),
        ),
        in_specs=[vmem] * 2,
        out_specs=(vmem, vmem),
        cost_estimate=pl.CostEstimate(
            flops=came.size, bytes_accessed=came.size * 4, transcendentals=0
        ),
        compiler_params=pltpu.CompilerParams(vmem_limit_bytes=24 << 20),
        name="pack",
    )(came, modes_panel)


def update_kernel(turns, factor_ref, rhs_ref, *rest):
    count = 2 * len(turns)
    blocks, rest = rest[:count], rest[count:]
    if len(rest) == 1:
        (out_ref,) = rest
    else:
        modal_ref, back_ref, summed_ref, out_ref, forces_ref, panel_ref = rest
        forces_ref[...] = modal_ref[...] + back_ref[...]
        panel_ref[...] = summed_ref[: panel_ref.shape[0], :]
    width = out_ref.shape[2]
    depth = 2 * width
    rows = factor_ref.shape[1]
    y = lax.axis_index("y")
    core = lax.axis_index("core")
    pieces = []
    for j, block_ref in enumerate(blocks):
        source = core if j % 2 == 0 else 1 - core
        low, high = turns[j // 2]
        place = jnp.bitwise_xor(y, low + (high - low) * source) * 2 + source
        columns = pl.ds(pl.multiple_of(place * depth, depth), depth)
        straight = block_ref[:depth, :]
        crossed = jnp.concatenate([-straight[:, width:], straight[:, :width]], axis=1)
        pieces.append((columns, straight, crossed))
    for at in range(0, rows, CHUNK):
        span = slice(at, at + CHUNK)
        product = jnp.zeros((CHUNK, depth), F32)
        for columns, straight, crossed in pieces:
            product += jnp.dot(factor_ref[0, span, columns], straight, preferred_element_type=F32)
            product += jnp.dot(factor_ref[1, span, columns], crossed, preferred_element_type=F32)
        out_ref[0, span, :] = rhs_ref[0, span, :] - product[:, :width]
        out_ref[1, span, :] = rhs_ref[1, span, :] - product[:, width:]


def update(turns, factor_slab, rhs, blocks, name, others=()):
    depth = 2 * rhs.shape[2]
    rows = factor_slab.shape[1]
    vmem = pl.BlockSpec(memory_space=pltpu.VMEM)
    shapes = [jax.ShapeDtypeStruct(rhs.shape, F32)]
    if others:
        modal, _, summed = others
        shapes.append(jax.ShapeDtypeStruct(modal.shape, F32))
        shapes.append(jax.ShapeDtypeStruct((summed.shape[0] * 2 // 3, summed.shape[1]), F32))
    return pl.pallas_call(
        functools.partial(update_kernel, turns),
        out_shape=shapes,
        in_specs=[vmem] * (2 + len(blocks) + len(others)),
        out_specs=[vmem] * len(shapes),
        cost_estimate=pl.CostEstimate(
            flops=len(blocks) * 4 * rows * depth * 2 * rhs.shape[2],
            bytes_accessed=len(blocks) * 4 * rows * depth,
            transcendentals=0,
        ),
        compiler_params=pltpu.CompilerParams(vmem_limit_bytes=24 << 20),
        name=name,
    )(factor_slab, rhs, *blocks, *others)


def on_device(
    diag_inverse, panel_rhs, factor_slab, pending_rhs, solved_prev, modes_prev, modes_panel
):
    width = panel_rhs.shape[2]
    own = modes_panel.shape[0]
    peers = diag_inverse.shape[1] // own
    outgoing = first_partials(diag_inverse, panel_rhs, modes_prev, solved_prev, peers, own)
    came = lax.all_to_all(outgoing, COL, 0, 0, tiled=True)
    summed, packed = pack(came, modes_panel.astype(F32))
    gathered = lax.all_to_all(packed, COL, 0, 0, tiled=True)
    block = jnp.concatenate(
        [
            gathered[:, :own].reshape(peers * own, width),
            gathered[:, own : 2 * own].reshape(peers * own, width),
        ],
        axis=1,
    )
    twin = swapped(block)
    modes_block = gathered[:, 2 * own : 3 * own].reshape(peers * own, width)
    share = gathered[:, 3 * own : 4 * own].astype(F32) + gathered[:, 4 * own :].astype(F32)
    latest = lax.dot_general(
        modes_block, block, (((0,), (0,)), ((), ())), preferred_element_type=F32
    )
    share = share.reshape(2, width, width) + jnp.stack([latest[:, :width], latest[:, width:]])
    modal = split(share.reshape(2 * width, width))
    sent = jnp.concatenate([block, modal], axis=0)
    head = flipped(sent, EARLY[0])
    tail = [flipped(sent, turn) for turn in LATE]
    depth = block.shape[0]
    (started,) = update(OWN, factor_slab, pending_rhs, [block, twin], "update_own")
    (started,) = update(
        EARLY, factor_slab, started, [head, swapped(head[:depth])], "update_early"
    )
    started, tail = lax.optimization_barrier((started, tail))
    twins = [swapped(c[:depth]) for c in tail]
    first, third, second = (joined(c[depth:]) for c in (*tail, head))
    modal = (joined(modal) + second) + (first + third)
    updated_rhs, modal_forces, panel_solution = update(
        LATE,
        factor_slab,
        started,
        [b for two in zip(tail, twins) for b in two],
        "update_late",
        (modal, swapped(modal), summed),
    )
    modal_forces = modal_forces.reshape(2, width, width)
    panel_solution = panel_solution.reshape(2, own, width)
    return (panel_solution, updated_rhs, modal_forces)


def solution(mesh):
    fine = Mesh(mesh.devices.reshape(4, 2, 8, 4), ("y", "core", "z", "x"))
    row = ("y", "core")
    every = ("y", "core", "z", "x")
    placed = (
        P(None, row, COL),
        P(None, COL, None),
        P(None, every, None),
        P(None, every, None),
        P(None, every, None),
        P(every, None),
        P(every, None),
    )
    return jax.shard_map(
        on_device,
        mesh=fine,
        in_specs=placed,
        out_specs=(P(None, every, None), P(None, every, None), P()),
        check_vma=False,
    )
```

```python
import functools

import jax
import jax.numpy as jnp
from jax import lax
from jax.experimental import pallas as pl
from jax.experimental.pallas import tpu as pltpu
from jax.sharding import Mesh, PartitionSpec as P

F32 = jnp.float32
BF16 = jnp.bfloat16
COL = ("z", "x")
SWAP = [(0, 1), (1, 0)]
CHUNK = 128
OWN = (((0, 0), 0),)
EARLY = (((0, 0), 1), ((2, 2), 0), ((2, 2), 1))
LATE = (((1, 3), 0), ((1, 3), 1), ((3, 1), 0), ((3, 1), 1))


def swapped(value):
    return lax.ppermute(value, "core", SWAP)


def flipped(value, turn):
    pairs = [(2 * y + core, 2 * (y ^ turn[core]) + core) for y in range(4) for core in range(2)]
    return lax.ppermute(value, ("y", "core"), pairs)


def split(value):
    high = lax.reduce_precision(value, 8, 7)
    return jnp.concatenate([high.astype(BF16), (value - high).astype(BF16)], axis=1)


def joined(pair):
    width = pair.shape[1] // 2
    return pair[:, :width].astype(F32) + pair[:, width:].astype(F32)


def first_kernel(diag_hbm, rhs_hbm, modes_hbm, solved_hbm, out_ref, diag_ref, rhs_ref, modes_ref, solved_ref, sems):
    peers, rows, width = out_ref.shape
    own = rows // 3
    moves = [
        pltpu.make_async_copy(source, target, sems.at[i])
        for i, (source, target) in enumerate(
            (
                (modes_hbm, modes_ref),
                (solved_hbm, solved_ref),
                (rhs_hbm, rhs_ref),
                (diag_hbm, diag_ref),
            )
        )
    ]
    for move in moves:
        move.start()
    over_first = (((0,), (0,)), ((), ()))
    half = peers // 2
    moves[0].wait()
    moves[1].wait()
    for c in range(2):
        earlier = lax.dot_general(
            modes_ref[...], solved_ref[c], over_first, preferred_element_type=F32
        )
        out_ref[c * half : (c + 1) * half, 2 * own :, :] = earlier.reshape(half, own, width)
    moves[2].wait()
    moves[3].wait()
    left = jnp.concatenate([diag_ref[0], diag_ref[1]], axis=0)
    real, imag = rhs_ref[0], rhs_ref[1]
    right = jnp.concatenate(
        [jnp.concatenate([real, imag], axis=1), jnp.concatenate([-imag, real], axis=1)], axis=0
    )
    partial = lax.dot_general(
        left, right, over_first, precision=lax.Precision.HIGHEST, preferred_element_type=F32
    )
    out_ref[:, :own, :] = partial[:, :width].reshape(peers, own, width)
    out_ref[:, own : 2 * own, :] = partial[:, width:].reshape(peers, own, width)


def first_partials(diag_inverse, panel_rhs, modes_prev, solved_prev, peers, own):
    width = panel_rhs.shape[2]
    args = (jnp.swapaxes(diag_inverse, 1, 2), panel_rhs, modes_prev, solved_prev)
    return pl.pallas_call(
        first_kernel,
        out_shape=jax.ShapeDtypeStruct((peers, 3 * own, width), F32),
        in_specs=[pl.BlockSpec(memory_space=pltpu.HBM)] * 4,
        out_specs=pl.BlockSpec(memory_space=pltpu.VMEM),
        scratch_shapes=[pltpu.VMEM(a.shape, a.dtype) for a in args]
        + [pltpu.SemaphoreType.DMA((4,))],
        name="partials",
    )(*args)


def pack_kernel(came_ref, modes_ref, panel_ref, packed_ref):
    own = modes_ref.shape[0]
    summed = jnp.sum(came_ref[...], axis=0)
    panel_ref[...] = summed
    share = summed[2 * own :]
    high = share.astype(BF16).astype(F32)
    rows = jnp.concatenate(
        [summed[: 2 * own], modes_ref[...], high, share - high], axis=0
    )
    packed_ref[...] = jnp.broadcast_to(rows.astype(BF16)[None], packed_ref.shape)


def pack(came, modes_panel):
    peers, rows, width = came.shape
    own = rows // 3
    vmem = pl.BlockSpec(memory_space=pltpu.VMEM)
    return pl.pallas_call(
        pack_kernel,
        out_shape=(
            jax.ShapeDtypeStruct((3 * own, width), F32),
            jax.ShapeDtypeStruct((peers, 5 * own, width), BF16),
        ),
        in_specs=[vmem] * 2,
        out_specs=(vmem, vmem),
        cost_estimate=pl.CostEstimate(
            flops=came.size, bytes_accessed=came.size * 4, transcendentals=0
        ),
        compiler_params=pltpu.CompilerParams(vmem_limit_bytes=24 << 20),
        name="pack",
    )(came, modes_panel)


def update_kernel(turns, factor_ref, rhs_ref, *rest):
    count = len(turns)
    blocks, rest = rest[:count], rest[count:]
    if len(rest) == 1:
        (out_ref,) = rest
    else:
        modal_ref, back_ref, summed_ref, out_ref, forces_ref, panel_ref = rest
        forces_ref[...] = modal_ref[...] + back_ref[...]
        panel_ref[...] = summed_ref[: panel_ref.shape[0], :]
    width = out_ref.shape[2]
    depth = 2 * width
    rows = factor_ref.shape[1]
    y = lax.axis_index("y")
    core = lax.axis_index("core")
    pieces = []
    for j, block_ref in enumerate(blocks):
        (low, high), other = turns[j]
        source = 1 - core if other else core
        place = jnp.bitwise_xor(y, low + (high - low) * source) * 2 + source
        columns = pl.ds(pl.multiple_of(place * depth, depth), depth)
        straight = block_ref[:depth, :]
        crossed = jnp.concatenate([-straight[:, width:], straight[:, :width]], axis=1)
        pieces.append((columns, straight, crossed))
    for at in range(0, rows, CHUNK):
        span = slice(at, at + CHUNK)
        product = jnp.zeros((CHUNK, depth), F32)
        for columns, straight, crossed in pieces:
            product += jnp.dot(factor_ref[0, span, columns], straight, preferred_element_type=F32)
            product += jnp.dot(factor_ref[1, span, columns], crossed, preferred_element_type=F32)
        out_ref[0, span, :] = rhs_ref[0, span, :] - product[:, :width]
        out_ref[1, span, :] = rhs_ref[1, span, :] - product[:, width:]


def update(turns, factor_slab, rhs, blocks, name, others=()):
    depth = 2 * rhs.shape[2]
    rows = factor_slab.shape[1]
    vmem = pl.BlockSpec(memory_space=pltpu.VMEM)
    shapes = [jax.ShapeDtypeStruct(rhs.shape, F32)]
    if others:
        modal, _, summed = others
        shapes.append(jax.ShapeDtypeStruct(modal.shape, F32))
        shapes.append(jax.ShapeDtypeStruct((summed.shape[0] * 2 // 3, summed.shape[1]), F32))
    return pl.pallas_call(
        functools.partial(update_kernel, turns),
        out_shape=shapes,
        in_specs=[vmem] * (2 + len(blocks) + len(others)),
        out_specs=[vmem] * len(shapes),
        cost_estimate=pl.CostEstimate(
            flops=len(blocks) * 4 * rows * depth * 2 * rhs.shape[2],
            bytes_accessed=len(blocks) * 4 * rows * depth,
            transcendentals=0,
        ),
        compiler_params=pltpu.CompilerParams(vmem_limit_bytes=24 << 20),
        name=name,
    )(factor_slab, rhs, *blocks, *others)


def on_device(
    diag_inverse, panel_rhs, factor_slab, pending_rhs, solved_prev, modes_prev, modes_panel
):
    width = panel_rhs.shape[2]
    own = modes_panel.shape[0]
    peers = diag_inverse.shape[1] // own
    outgoing = first_partials(diag_inverse, panel_rhs, modes_prev, solved_prev, peers, own)
    came = lax.all_to_all(outgoing, COL, 0, 0, tiled=True)
    summed, packed = pack(came, modes_panel.astype(F32))
    gathered = lax.all_to_all(packed, COL, 0, 0, tiled=True)
    block = jnp.concatenate(
        [
            gathered[:, :own].reshape(peers * own, width),
            gathered[:, own : 2 * own].reshape(peers * own, width),
        ],
        axis=1,
    )
    twin = swapped(block)
    modes_block = gathered[:, 2 * own : 3 * own].reshape(peers * own, width)
    share = gathered[:, 3 * own : 4 * own].astype(F32) + gathered[:, 4 * own :].astype(F32)
    latest = lax.dot_general(
        modes_block, block, (((0,), (0,)), ((), ())), preferred_element_type=F32
    )
    share = share.reshape(2, width, width) + jnp.stack([latest[:, :width], latest[:, width:]])
    modal = split(share.reshape(2 * width, width))
    sent = jnp.concatenate([block, modal], axis=0)
    head = flipped(sent, EARLY[1][0])
    tail = [flipped(sent, turn) for turn, other in LATE if not other]
    depth = block.shape[0]
    (started,) = update(OWN, factor_slab, pending_rhs, [block], "update_own")
    started, head = lax.optimization_barrier((started, head))
    (started,) = update(
        EARLY, factor_slab, started, [twin, head, swapped(head[:depth])], "update_early"
    )
    started, tail = lax.optimization_barrier((started, tail))
    twins = [swapped(c[:depth]) for c in tail]
    first, third, second = (joined(c[depth:]) for c in (*tail, head))
    modal = (joined(modal) + second) + (first + third)
    updated_rhs, modal_forces, panel_solution = update(
        LATE,
        factor_slab,
        started,
        [b for two in zip(tail, twins) for b in two],
        "update_late",
        (modal, swapped(modal), summed),
    )
    modal_forces = modal_forces.reshape(2, width, width)
    panel_solution = panel_solution.reshape(2, own, width)
    return (panel_solution, updated_rhs, modal_forces)


def solution(mesh):
    fine = Mesh(mesh.devices.reshape(4, 2, 8, 4), ("y", "core", "z", "x"))
    row = ("y", "core")
    every = ("y", "core", "z", "x")
    placed = (
        P(None, row, COL),
        P(None, COL, None),
        P(None, every, None),
        P(None, every, None),
        P(None, every, None),
        P(every, None),
        P(every, None),
    )
    return jax.shard_map(
        on_device,
        mesh=fine,
        in_specs=placed,
        out_specs=(P(None, every, None), P(None, every, None), P()),
        check_vma=False,
    )
```

```python
import functools

import jax
import jax.numpy as jnp
from jax import lax
from jax.experimental import pallas as pl
from jax.experimental.pallas import tpu as pltpu
from jax.sharding import Mesh, PartitionSpec as P

F32 = jnp.float32
BF16 = jnp.bfloat16
COL = ("z", "x")
SWAP = [(0, 1), (1, 0)]
CHUNK = 128
OWN = (((0, 0), 0),)
EARLY = (((0, 0), 1), ((1, 3), 0), ((1, 3), 1))
LATE = (((3, 1), 0), ((3, 1), 1), ((2, 2), 0), ((2, 2), 1))


def swapped(value):
    return lax.ppermute(value, "core", SWAP)


def flipped(value, turn):
    pairs = [(2 * y + core, 2 * (y ^ turn[core]) + core) for y in range(4) for core in range(2)]
    return lax.ppermute(value, ("y", "core"), pairs)


def split(value):
    high = lax.reduce_precision(value, 8, 7)
    return jnp.concatenate([high.astype(BF16), (value - high).astype(BF16)], axis=1)


def joined(pair):
    width = pair.shape[1] // 2
    return pair[:, :width].astype(F32) + pair[:, width:].astype(F32)


def first_kernel(diag_hbm, rhs_hbm, modes_hbm, solved_hbm, out_ref, diag_ref, rhs_ref, modes_ref, solved_ref, sems):
    peers, rows, width = out_ref.shape
    own = rows // 3
    moves = [
        pltpu.make_async_copy(source, target, sems.at[i])
        for i, (source, target) in enumerate(
            (
                (modes_hbm, modes_ref),
                (solved_hbm, solved_ref),
                (rhs_hbm, rhs_ref),
                (diag_hbm, diag_ref),
            )
        )
    ]
    for move in moves:
        move.start()
    over_first = (((0,), (0,)), ((), ()))
    half = peers // 2
    moves[0].wait()
    moves[1].wait()
    for c in range(2):
        earlier = lax.dot_general(
            modes_ref[...], solved_ref[c], over_first, preferred_element_type=F32
        )
        out_ref[c * half : (c + 1) * half, 2 * own :, :] = earlier.reshape(half, own, width)
    moves[2].wait()
    moves[3].wait()
    left = jnp.concatenate([diag_ref[0], diag_ref[1]], axis=0)
    real, imag = rhs_ref[0], rhs_ref[1]
    right = jnp.concatenate(
        [jnp.concatenate([real, imag], axis=1), jnp.concatenate([-imag, real], axis=1)], axis=0
    )
    partial = lax.dot_general(
        left, right, over_first, precision=lax.Precision.HIGHEST, preferred_element_type=F32
    )
    out_ref[:, :own, :] = partial[:, :width].reshape(peers, own, width)
    out_ref[:, own : 2 * own, :] = partial[:, width:].reshape(peers, own, width)


def first_partials(diag_inverse, panel_rhs, modes_prev, solved_prev, peers, own):
    width = panel_rhs.shape[2]
    args = (jnp.swapaxes(diag_inverse, 1, 2), panel_rhs, modes_prev, solved_prev)
    return pl.pallas_call(
        first_kernel,
        out_shape=jax.ShapeDtypeStruct((peers, 3 * own, width), F32),
        in_specs=[pl.BlockSpec(memory_space=pltpu.HBM)] * 4,
        out_specs=pl.BlockSpec(memory_space=pltpu.VMEM),
        scratch_shapes=[pltpu.VMEM(a.shape, a.dtype) for a in args]
        + [pltpu.SemaphoreType.DMA((4,))],
        name="partials",
    )(*args)


def pack_kernel(came_ref, modes_ref, panel_ref, packed_ref):
    own = modes_ref.shape[0]
    summed = jnp.sum(came_ref[...], axis=0)
    panel_ref[...] = summed
    share = summed[2 * own :]
    high = share.astype(BF16).astype(F32)
    rows = jnp.concatenate(
        [summed[: 2 * own], modes_ref[...], high, share - high], axis=0
    )
    packed_ref[...] = jnp.broadcast_to(rows.astype(BF16)[None], packed_ref.shape)


def pack(came, modes_panel):
    peers, rows, width = came.shape
    own = rows // 3
    vmem = pl.BlockSpec(memory_space=pltpu.VMEM)
    return pl.pallas_call(
        pack_kernel,
        out_shape=(
            jax.ShapeDtypeStruct((3 * own, width), F32),
            jax.ShapeDtypeStruct((peers, 5 * own, width), BF16),
        ),
        in_specs=[vmem] * 2,
        out_specs=(vmem, vmem),
        cost_estimate=pl.CostEstimate(
            flops=came.size, bytes_accessed=came.size * 4, transcendentals=0
        ),
        compiler_params=pltpu.CompilerParams(vmem_limit_bytes=24 << 20),
        name="pack",
    )(came, modes_panel)


def update_kernel(turns, factor_ref, rhs_ref, *rest):
    count = len(turns)
    blocks, rest = rest[:count], rest[count:]
    if len(rest) == 1:
        (out_ref,) = rest
    else:
        modal_ref, back_ref, summed_ref, out_ref, forces_ref, panel_ref = rest
        forces_ref[...] = modal_ref[...] + back_ref[...]
        panel_ref[...] = summed_ref[: panel_ref.shape[0], :]
    width = out_ref.shape[2]
    depth = 2 * width
    rows = factor_ref.shape[1]
    y = lax.axis_index("y")
    core = lax.axis_index("core")
    pieces = []
    for j, block_ref in enumerate(blocks):
        (low, high), other = turns[j]
        source = 1 - core if other else core
        place = jnp.bitwise_xor(y, low + (high - low) * source) * 2 + source
        columns = pl.ds(pl.multiple_of(place * depth, depth), depth)
        straight = block_ref[:depth, :]
        crossed = jnp.concatenate([-straight[:, width:], straight[:, :width]], axis=1)
        pieces.append((columns, straight, crossed))
    for at in range(0, rows, CHUNK):
        span = slice(at, at + CHUNK)
        product = jnp.zeros((CHUNK, depth), F32)
        for columns, straight, crossed in pieces:
            product += jnp.dot(factor_ref[0, span, columns], straight, preferred_element_type=F32)
            product += jnp.dot(factor_ref[1, span, columns], crossed, preferred_element_type=F32)
        out_ref[0, span, :] = rhs_ref[0, span, :] - product[:, :width]
        out_ref[1, span, :] = rhs_ref[1, span, :] - product[:, width:]


def update(turns, factor_slab, rhs, blocks, name, others=()):
    depth = 2 * rhs.shape[2]
    rows = factor_slab.shape[1]
    vmem = pl.BlockSpec(memory_space=pltpu.VMEM)
    shapes = [jax.ShapeDtypeStruct(rhs.shape, F32)]
    if others:
        modal, _, summed = others
        shapes.append(jax.ShapeDtypeStruct(modal.shape, F32))
        shapes.append(jax.ShapeDtypeStruct((summed.shape[0] * 2 // 3, summed.shape[1]), F32))
    return pl.pallas_call(
        functools.partial(update_kernel, turns),
        out_shape=shapes,
        in_specs=[vmem] * (2 + len(blocks) + len(others)),
        out_specs=[vmem] * len(shapes),
        cost_estimate=pl.CostEstimate(
            flops=len(blocks) * 4 * rows * depth * 2 * rhs.shape[2],
            bytes_accessed=len(blocks) * 4 * rows * depth,
            transcendentals=0,
        ),
        compiler_params=pltpu.CompilerParams(vmem_limit_bytes=24 << 20),
        name=name,
    )(factor_slab, rhs, *blocks, *others)


def on_device(
    diag_inverse, panel_rhs, factor_slab, pending_rhs, solved_prev, modes_prev, modes_panel
):
    width = panel_rhs.shape[2]
    own = modes_panel.shape[0]
    peers = diag_inverse.shape[1] // own
    outgoing = first_partials(diag_inverse, panel_rhs, modes_prev, solved_prev, peers, own)
    came = lax.all_to_all(outgoing, COL, 0, 0, tiled=True)
    summed, packed = pack(came, modes_panel.astype(F32))
    gathered = lax.all_to_all(packed, COL, 0, 0, tiled=True)
    block = jnp.concatenate(
        [
            gathered[:, :own].reshape(peers * own, width),
            gathered[:, own : 2 * own].reshape(peers * own, width),
        ],
        axis=1,
    )
    twin = swapped(block)
    modes_block = gathered[:, 2 * own : 3 * own].reshape(peers * own, width)
    share = gathered[:, 3 * own : 4 * own].astype(F32) + gathered[:, 4 * own :].astype(F32)
    latest = lax.dot_general(
        modes_block, block, (((0,), (0,)), ((), ())), preferred_element_type=F32
    )
    share = share.reshape(2, width, width) + jnp.stack([latest[:, :width], latest[:, width:]])
    modal = split(share.reshape(2 * width, width))
    sent = jnp.concatenate([block, modal], axis=0)
    head = flipped(sent, EARLY[1][0])
    tail = [flipped(sent, turn) for turn, other in LATE if not other]
    depth = block.shape[0]
    (started,) = update(OWN, factor_slab, pending_rhs, [block], "update_own")
    started, head = lax.optimization_barrier((started, head))
    (started,) = update(
        EARLY, factor_slab, started, [twin, head, swapped(head[:depth])], "update_early"
    )
    started, tail = lax.optimization_barrier((started, tail))
    twins = [swapped(c[:depth]) for c in tail]
    first, third, second = (joined(c[depth:]) for c in (head, *tail))
    modal = (joined(modal) + second) + (first + third)
    updated_rhs, modal_forces, panel_solution = update(
        LATE,
        factor_slab,
        started,
        [b for two in zip(tail, twins) for b in two],
        "update_late",
        (modal, swapped(modal), summed),
    )
    modal_forces = modal_forces.reshape(2, width, width)
    panel_solution = panel_solution.reshape(2, own, width)
    return (panel_solution, updated_rhs, modal_forces)


def solution(mesh):
    fine = Mesh(mesh.devices.reshape(4, 2, 8, 4), ("y", "core", "z", "x"))
    row = ("y", "core")
    every = ("y", "core", "z", "x")
    placed = (
        P(None, row, COL),
        P(None, COL, None),
        P(None, every, None),
        P(None, every, None),
        P(None, every, None),
        P(every, None),
        P(every, None),
    )
    return jax.shard_map(
        on_device,
        mesh=fine,
        in_specs=placed,
        out_specs=(P(None, every, None), P(None, every, None), P()),
        check_vma=False,
    )
```

```python
import functools

import jax
import jax.numpy as jnp
from jax import lax
from jax.experimental import pallas as pl
from jax.experimental.pallas import tpu as pltpu
from jax.sharding import Mesh, PartitionSpec as P

F32 = jnp.float32
BF16 = jnp.bfloat16
COL = ("z", "x")
SWAP = [(0, 1), (1, 0)]
CHUNK = 128
OWN = (((0, 0), 0),)
EARLY = (((0, 0), 1), ((2, 2), 0), ((2, 2), 1))
LATE = (((1, 3), 0), ((1, 3), 1), ((3, 1), 0), ((3, 1), 1))


def swapped(value):
    return lax.ppermute(value, "core", SWAP)


def flipped(value, turn):
    pairs = [(2 * y + core, 2 * (y ^ turn[core]) + core) for y in range(4) for core in range(2)]
    return lax.ppermute(value, ("y", "core"), pairs)


def split(value):
    high = lax.reduce_precision(value, 8, 7)
    return jnp.concatenate([high.astype(BF16), (value - high).astype(BF16)], axis=1)


def joined(pair):
    width = pair.shape[1] // 2
    return pair[:, :width].astype(F32) + pair[:, width:].astype(F32)


def first_kernel(diag_hbm, rhs_hbm, modes_hbm, solved_hbm, out_ref, diag_ref, rhs_ref, modes_ref, solved_ref, sems):
    peers, rows, width = out_ref.shape
    own = rows // 3
    moves = [
        pltpu.make_async_copy(source, target, sems.at[i])
        for i, (source, target) in enumerate(
            (
                (diag_hbm, diag_ref),
                (rhs_hbm, rhs_ref),
                (modes_hbm, modes_ref),
                (solved_hbm, solved_ref),
            )
        )
    ]
    for move in moves:
        move.start()
    over_first = (((0,), (0,)), ((), ()))
    half = peers // 2
    moves[0].wait()
    moves[1].wait()
    left = jnp.concatenate([diag_ref[0], diag_ref[1]], axis=0)
    real, imag = rhs_ref[0], rhs_ref[1]
    right = jnp.concatenate(
        [jnp.concatenate([real, imag], axis=1), jnp.concatenate([-imag, real], axis=1)], axis=0
    )
    partial = lax.dot_general(
        left, right, over_first, precision=lax.Precision.HIGHEST, preferred_element_type=F32
    )
    out_ref[:, :own, :] = partial[:, :width].reshape(peers, own, width)
    out_ref[:, own : 2 * own, :] = partial[:, width:].reshape(peers, own, width)
    moves[2].wait()
    moves[3].wait()
    for c in range(2):
        earlier = lax.dot_general(
            modes_ref[...], solved_ref[c], over_first, preferred_element_type=F32
        )
        out_ref[c * half : (c + 1) * half, 2 * own :, :] = earlier.reshape(half, own, width)


def first_partials(diag_inverse, panel_rhs, modes_prev, solved_prev, peers, own):
    width = panel_rhs.shape[2]
    args = (jnp.swapaxes(diag_inverse, 1, 2), panel_rhs, modes_prev, solved_prev)
    return pl.pallas_call(
        first_kernel,
        out_shape=jax.ShapeDtypeStruct((peers, 3 * own, width), F32),
        in_specs=[pl.BlockSpec(memory_space=pltpu.HBM)] * 4,
        out_specs=pl.BlockSpec(memory_space=pltpu.VMEM),
        scratch_shapes=[pltpu.VMEM(a.shape, a.dtype) for a in args]
        + [pltpu.SemaphoreType.DMA((4,))],
        name="partials",
    )(*args)


def pack_kernel(came_ref, modes_ref, panel_ref, packed_ref):
    own = modes_ref.shape[0]
    summed = jnp.sum(came_ref[...], axis=0)
    panel_ref[...] = summed
    share = summed[2 * own :]
    high = share.astype(BF16).astype(F32)
    rows = jnp.concatenate(
        [summed[: 2 * own], modes_ref[...], high, share - high], axis=0
    )
    packed_ref[...] = jnp.broadcast_to(rows.astype(BF16)[None], packed_ref.shape)


def pack(came, modes_panel):
    peers, rows, width = came.shape
    own = rows // 3
    vmem = pl.BlockSpec(memory_space=pltpu.VMEM)
    return pl.pallas_call(
        pack_kernel,
        out_shape=(
            jax.ShapeDtypeStruct((3 * own, width), F32),
            jax.ShapeDtypeStruct((peers, 5 * own, width), BF16),
        ),
        in_specs=[vmem] * 2,
        out_specs=(vmem, vmem),
        cost_estimate=pl.CostEstimate(
            flops=came.size, bytes_accessed=came.size * 4, transcendentals=0
        ),
        compiler_params=pltpu.CompilerParams(vmem_limit_bytes=24 << 20),
        name="pack",
    )(came, modes_panel)


def update_kernel(turns, factor_ref, rhs_ref, *rest):
    count = len(turns)
    blocks, rest = rest[:count], rest[count:]
    if len(rest) == 1:
        (out_ref,) = rest
    else:
        modal_ref, back_ref, summed_ref, out_ref, forces_ref, panel_ref = rest
        forces_ref[...] = modal_ref[...] + back_ref[...]
        panel_ref[...] = summed_ref[: panel_ref.shape[0], :]
    width = out_ref.shape[2]
    depth = 2 * width
    rows = factor_ref.shape[1]
    y = lax.axis_index("y")
    core = lax.axis_index("core")
    pieces = []
    for j, block_ref in enumerate(blocks):
        (low, high), other = turns[j]
        source = 1 - core if other else core
        place = jnp.bitwise_xor(y, low + (high - low) * source) * 2 + source
        columns = pl.ds(pl.multiple_of(place * depth, depth), depth)
        straight = block_ref[:depth, :]
        crossed = jnp.concatenate([-straight[:, width:], straight[:, :width]], axis=1)
        pieces.append((columns, straight, crossed))
    for at in range(0, rows, CHUNK):
        span = slice(at, at + CHUNK)
        product = jnp.zeros((CHUNK, depth), F32)
        for columns, straight, crossed in pieces:
            product += jnp.dot(factor_ref[0, span, columns], straight, preferred_element_type=F32)
            product += jnp.dot(factor_ref[1, span, columns], crossed, preferred_element_type=F32)
        out_ref[0, span, :] = rhs_ref[0, span, :] - product[:, :width]
        out_ref[1, span, :] = rhs_ref[1, span, :] - product[:, width:]


def update(turns, factor_slab, rhs, blocks, name, others=()):
    depth = 2 * rhs.shape[2]
    rows = factor_slab.shape[1]
    vmem = pl.BlockSpec(memory_space=pltpu.VMEM)
    shapes = [jax.ShapeDtypeStruct(rhs.shape, F32)]
    if others:
        modal, _, summed = others
        shapes.append(jax.ShapeDtypeStruct(modal.shape, F32))
        shapes.append(jax.ShapeDtypeStruct((summed.shape[0] * 2 // 3, summed.shape[1]), F32))
    return pl.pallas_call(
        functools.partial(update_kernel, turns),
        out_shape=shapes,
        in_specs=[vmem] * (2 + len(blocks) + len(others)),
        out_specs=[vmem] * len(shapes),
        cost_estimate=pl.CostEstimate(
            flops=len(blocks) * 4 * rows * depth * 2 * rhs.shape[2],
            bytes_accessed=len(blocks) * 4 * rows * depth,
            transcendentals=0,
        ),
        compiler_params=pltpu.CompilerParams(vmem_limit_bytes=24 << 20),
        name=name,
    )(factor_slab, rhs, *blocks, *others)


def on_device(
    diag_inverse, panel_rhs, factor_slab, pending_rhs, solved_prev, modes_prev, modes_panel
):
    width = panel_rhs.shape[2]
    own = modes_panel.shape[0]
    peers = diag_inverse.shape[1] // own
    outgoing = first_partials(diag_inverse, panel_rhs, modes_prev, solved_prev, peers, own)
    came = lax.all_to_all(outgoing, COL, 0, 0, tiled=True)
    summed, packed = pack(came, modes_panel.astype(F32))
    gathered = lax.all_to_all(packed, COL, 0, 0, tiled=True)
    block = jnp.concatenate(
        [
            gathered[:, :own].reshape(peers * own, width),
            gathered[:, own : 2 * own].reshape(peers * own, width),
        ],
        axis=1,
    )
    twin = swapped(block)
    modes_block = gathered[:, 2 * own : 3 * own].reshape(peers * own, width)
    share = gathered[:, 3 * own : 4 * own].astype(F32) + gathered[:, 4 * own :].astype(F32)
    latest = lax.dot_general(
        modes_block, block, (((0,), (0,)), ((), ())), preferred_element_type=F32
    )
    share = share.reshape(2, width, width) + jnp.stack([latest[:, :width], latest[:, width:]])
    modal = split(share.reshape(2 * width, width))
    sent = jnp.concatenate([block, modal], axis=0)
    head = flipped(sent, EARLY[1][0])
    tail = [flipped(sent, turn) for turn, other in LATE if not other]
    depth = block.shape[0]
    (started,) = update(OWN, factor_slab, pending_rhs, [block], "update_own")
    started, head = lax.optimization_barrier((started, head))
    (started,) = update(
        EARLY, factor_slab, started, [twin, head, swapped(head[:depth])], "update_early"
    )
    started, tail = lax.optimization_barrier((started, tail))
    twins = [swapped(c[:depth]) for c in tail]
    first, third, second = (joined(c[depth:]) for c in (*tail, head))
    modal = (joined(modal) + second) + (first + third)
    updated_rhs, modal_forces, panel_solution = update(
        LATE,
        factor_slab,
        started,
        [b for two in zip(tail, twins) for b in two],
        "update_late",
        (modal, swapped(modal), summed),
    )
    modal_forces = modal_forces.reshape(2, width, width)
    panel_solution = panel_solution.reshape(2, own, width)
    return (panel_solution, updated_rhs, modal_forces)


def solution(mesh):
    fine = Mesh(mesh.devices.reshape(4, 2, 8, 4), ("y", "core", "z", "x"))
    row = ("y", "core")
    every = ("y", "core", "z", "x")
    placed = (
        P(None, row, COL),
        P(None, COL, None),
        P(None, every, None),
        P(None, every, None),
        P(None, every, None),
        P(every, None),
        P(every, None),
    )
    return jax.shard_map(
        on_device,
        mesh=fine,
        in_specs=placed,
        out_specs=(P(None, every, None), P(None, every, None), P()),
        check_vma=False,
    )
```
